256 devices in a mesh: dp: 16 (over x_hi, y, core), seq: 16 (over z, x_lo).
Axes of the slice: x: 4 (x_hi: 2, x_lo: 2; x = x_hi * 2 + x_lo), y: 4, z: 8, core: 2. Of those that a mesh axis runs over, the one named last changes fastest.
Arguments:
- query_states: bfloat16 [16, 2048, 2048], P('dp', 'seq'), may hold values from -45 to 45
- key_states: bfloat16 [16, 2048, 2048], P('dp', 'seq'), may hold values from -30 to 30
- value_states: bfloat16 [16, 2048, 2048], P('dp', 'seq'), may hold values from -6 to 6
- out_grad: bfloat16 [16, 2048, 2048], P('dp', 'seq'), may hold values from -6 to 6
- doc_ids: int32 [16, 2048], P('dp', 'seq'), may hold values from 0 to 7, never falling along the last dimension, each value on 1 to 512 neighbouring positions
- query_gain: float32 [2048], replicated, may hold values from 0.375 to 6.25
- key_gain: float32 [2048], replicated, may hold values from 0.375 to 6.25
Outputs:
- query_grad: bfloat16 [16, 2048, 2048], P('dp', 'seq')
- key_grad: bfloat16 [16, 2048, 2048], P('dp', 'seq')
- value_grad: bfloat16 [16, 2048, 2048], P('dp', 'seq')
- query_gain_grad: float32 [2048], P('seq')
- key_gain_grad: float32 [2048], P('seq')
The draws below stay inside these ranges and needn't reach their ends.
Inputs may be any that keep to these rules, and one draw needn't show every extreme that they name: `doc_ids`: Non-decreasing along each sequence; each document holds 1 to 512 positions, one exactly that many.
All inputs are finite; a program needn't handle non-finite values.
Results may differ from the reference program's by a relative error of at most 0.012.
The reference program's roundings to bfloat16 on the way (of `q_norm`, `k_norm`, `prob_low` and `dscore`) count: a program that leaves them out, or rounds other values in their place, can miss the bound.
Values may be sent and summed in bfloat16 or wider, within the bound.
A program may use at most 64 MiB of HBM per device.

```python
import math
import jax
import jax.numpy as jnp
import numpy as np
from jax import lax

HH = 16
HD = 128
DOCS = 8
SEQ_LEN = 2048
BATCH = 16
FEATURES = 2048


def scaled_normal(key, low, high):
    shape = (BATCH, SEQ_LEN, HH, HD)
    first, second, third = jax.random.split(key, 3)
    values = jnp.clip(jax.random.normal(first, shape, jnp.float32), -5.0, 5.0)
    row_scale = jnp.exp(jax.random.uniform(second, (BATCH, SEQ_LEN, HH, 1), jnp.float32, jnp.log(low), jnp.log(high)))
    col_scale = jnp.exp(jax.random.uniform(third, (1, 1, HH, HD), jnp.float32, jnp.log(0.5), jnp.log(2.0)))
    return values * row_scale * col_scale


def gain_levels(key, top):
    first, second = jax.random.split(key)
    level = jnp.exp(jax.random.uniform(first, (HH, 1), jnp.float32, jnp.log(0.5), jnp.log(top)))
    jitter = jax.random.uniform(second, (HH, HD), jnp.float32, 0.75, 1.25)
    return (level * jitter).reshape(HH * HD)


def draw_key_states(key, part):
    shared = scaled_normal(key, 0.3, 3.0)
    return shared.reshape(BATCH, SEQ_LEN, HH * HD).astype(jnp.bfloat16)


def draw_query_states(key, part):
    key = jax.random.fold_in(key, 1)
    own = scaled_normal(key, 0.3, 3.0)
    return own.reshape(BATCH, SEQ_LEN, HH * HD).astype(jnp.bfloat16)


def draw_query_gain(key, part):
    key = jax.random.fold_in(key, 3)
    return gain_levels(key, 2.5)


def draw_key_gain(key, part):
    key = jax.random.fold_in(key, 4)
    return gain_levels(key, 2.5)


def block_scale(own_key, extent, shards, smallest, largest):
    def one(dim, blocks):
        heights = jax.random.uniform(jax.random.fold_in(jax.random.fold_in(own_key, 6), dim), (blocks,), jnp.float32, smallest / len(shards), largest / len(shards))
        return jnp.repeat(jnp.exp(heights), extent[dim] // blocks).reshape((-1,) + (1,) * (len(extent) - dim - 1))

    level = one(*shards[0])
    for cut in shards[1:]:
        level = level * one(*cut)
    return level


def split_up(count, total, limit, skew):
    portions = [(1 << 20) // math.isqrt(grade ** skew) + 1 for grade in range(2, count + 1)]
    rest, counts = total - limit - (count - 1), [1] * (count - 1)
    while rest > 0:
        free = [i for i in range(count - 1) if counts[i] < limit]
        whole, budget = sum([portions[i] for i in free]), rest
        for i in free:
            extra = min(limit - counts[i], max(1, budget * portions[i] // whole), rest)
            counts[i] = counts[i] + extra
            rest = rest - extra
    return np.array([limit] + counts)


def uneven_parts(own_key, number_of, total, most, slope):
    if number_of == 2:
        one = jax.random.randint(own_key, (), max(1, total - most), min(most, total - 1) + 1)
        return jnp.stack([one, total - one])
    tallies = jnp.asarray(split_up(number_of, total, most, slope), jnp.int32)
    twos = (number_of - 1) // 2
    giver, receiver = tallies[1:1 + 2 * twos:2], tallies[2:2 + 2 * twos:2]
    slack = jnp.minimum(giver - 1, most - receiver)
    moved = jax.random.randint(jax.random.fold_in(own_key, 1), (twos,), 0, 1 << 20) % (slack + 1)
    tallies = tallies.at[1:1 + 2 * twos:2].set(giver - moved).at[2:2 + 2 * twos:2].set(receiver + moved)
    return tallies[jax.random.permutation(jax.random.fold_in(own_key, 2), number_of)]


def bell_draw(own_key, extent, scale, bound, pieces=(), kind=jnp.bfloat16):
    factor_of = block_scale(own_key, extent, pieces, -0.22, 0.18) if pieces else 1.0
    entries = jax.random.normal(own_key, extent, jnp.float32) * scale * factor_of
    return jnp.minimum(jnp.maximum(entries, -bound), bound).astype(kind)


def setup_inputs(seed: int = 0) -> dict:
    splits = jax.random.split(jax.random.key(seed), 8)
    return {
        "query_states": draw_query_states(jax.random.fold_in(splits[7], 71), 0),
        "key_states": draw_key_states(jax.random.fold_in(splits[7], 71), 0),
        "value_states": bell_draw(splits[2], (BATCH, SEQ_LEN, FEATURES), 1.0, 6.0, ((0, 16), (1, 16))),
        "out_grad": bell_draw(splits[3], (BATCH, SEQ_LEN, FEATURES), 1.0, 6.0, ((0, 16), (1, 16))),
        "doc_ids": jax.vmap(lambda own: jnp.searchsorted(jnp.cumsum(uneven_parts(own, DOCS, SEQ_LEN, SEQ_LEN // 4, 1)), jnp.arange(SEQ_LEN), side="right"))(jax.random.split(splits[4], BATCH)).reshape((BATCH, SEQ_LEN)).astype(jnp.int32),
        "query_gain": draw_query_gain(jax.random.fold_in(splits[7], 71), 0),
        "key_gain": draw_key_gain(jax.random.fold_in(splits[7], 71), 0),
    }


EPS = 1e-06
MASKED = -1e+30

def normalize(values, norm_gain_weight):
    input_float_rows = values.astype(jnp.float32)
    inverse_root_mean = lax.rsqrt(lax.optimization_barrier(jnp.mean(input_float_rows * input_float_rows, axis=-1, keepdims=True)) + EPS)
    normalized_input = input_float_rows * inverse_root_mean
    return (normalized_input, inverse_root_mean, (normalized_input * norm_gain_weight).astype(jnp.bfloat16))

def norm_backward_pass(normalized_input, inverse_root_mean, norm_gain_weight, incoming_gradient):
    gain_scaled_gradient = incoming_gradient * norm_gain_weight
    input_gradient = inverse_root_mean * (gain_scaled_gradient - normalized_input * lax.optimization_barrier(jnp.mean(gain_scaled_gradient * normalized_input, axis=-1, keepdims=True)))
    return (input_gradient.astype(jnp.bfloat16), lax.optimization_barrier(jnp.sum(incoming_gradient * normalized_input, axis=0)))

def head_backward(query, keyrow, value, dout, gain_q, gain_k, segs):
    scale = HD ** (-0.5)
    q_hat, q_rec, q_norm = normalize(query, gain_q)
    k_hat, k_rec, k_norm = normalize(keyrow, gain_k)
    position = jnp.arange(SEQ_LEN, dtype=jnp.int32)
    allowed = (position[None, :] <= position[:, None]) & (segs[None, :] == segs[:, None])
    scores = jnp.dot(q_norm, k_norm.T, preferred_element_type=jnp.float32) * scale
    scores = jnp.where(allowed, scores, MASKED)
    peak = lax.optimization_barrier(jnp.max(scores, axis=1, keepdims=True))
    total = lax.optimization_barrier(jnp.sum(jnp.where(allowed, jnp.exp(scores - peak), 0.0), axis=1, keepdims=True))
    lse = peak + jnp.log(total)
    prob = jnp.where(allowed, jnp.exp(scores - lse), 0.0)
    attn = jnp.dot(prob, value.astype(jnp.float32), precision=lax.Precision.HIGHEST)
    delta = lax.optimization_barrier(jnp.sum(dout.astype(jnp.float32) * attn, axis=1, keepdims=True))
    prob_low = prob.astype(jnp.bfloat16)
    value_grad = jnp.dot(prob_low.T, dout, preferred_element_type=jnp.float32).astype(jnp.bfloat16)
    dprob = jnp.dot(dout, value.T, preferred_element_type=jnp.float32)
    dscore = (prob * (dprob - delta) * scale).astype(jnp.bfloat16)
    dq_norm = jnp.dot(dscore, k_norm, preferred_element_type=jnp.float32)
    dk_norm = jnp.dot(dscore.T, q_norm, preferred_element_type=jnp.float32)
    query_grad, gain_q_grad = norm_backward_pass(q_hat, q_rec, gain_q, dq_norm)
    key_grad, gain_k_grad = norm_backward_pass(k_hat, k_rec, gain_k, dk_norm)
    return (query_grad, key_grad, value_grad, gain_q_grad, gain_k_grad)

def reference(query_states, key_states, value_states, out_grad, doc_ids, query_gain, key_gain):

    def split(values):
        return values.reshape(BATCH, SEQ_LEN, HH, HD).transpose(0, 2, 1, 3)
    gains_q = query_gain.reshape(HH, HD)
    gains_k = key_gain.reshape(HH, HD)

    def per_sequence(item):
        query, keyrow, value, dout, segs = item

        def per_head(head_item):
            return head_backward(*head_item, segs)
        return lax.map(per_head, (query, keyrow, value, dout, gains_q, gains_k))
    results = lax.map(per_sequence, (split(query_states), split(key_states), split(value_states), split(out_grad), doc_ids))

    def joined(values):
        return values.transpose(0, 2, 1, 3).reshape(BATCH, SEQ_LEN, FEATURES)
    return (joined(results[0]), joined(results[1]), joined(results[2]), lax.optimization_barrier(jnp.sum(results[3], axis=0)).reshape(FEATURES), lax.optimization_barrier(jnp.sum(results[4], axis=0)).reshape(FEATURES))
```

```python
import functools

import jax
import jax.numpy as jnp
from jax import lax
from jax.experimental import pallas as pl
from jax.experimental.pallas import tpu as pltpu
from jax.sharding import PartitionSpec as P

HD = 128
EPS = 1e-06
MASKED = -1e30
LOG2E = 1.4426950408889634
SCALE = HD ** (-0.5)

BLOCK = 128
REACH = 4
SLOTS = REACH + 1
GROUP = 1
FORWARD, ACROSS, QUERIES, KEYS = 1, 2, 3, 4


def dot_nt(a, b):
    return lax.dot_general(a, b, (((1,), (1,)), ((), ())), preferred_element_type=jnp.float32)


def dot_nn(a, b):
    return lax.dot_general(a, b, (((1,), (0,)), ((), ())), preferred_element_type=jnp.float32)


def inverse_rms(x):
    return lax.rsqrt(jnp.mean(x * x, axis=-1, keepdims=True) + EPS)


def kernel(
    n_seq, n_dp, heads,
    q_ref, k_ref, v_ref, d_ref, doc_ref, gq_ref, gk_ref,
    dq_out, dk_out, dv_out, gq_out, gk_out,
    kvw, qdw, docw, statw, bias_q, bias_k, gsend, grecv, tsend, trecv,
    kv_s, kv_r, qd_s, qd_r, doc_s, doc_r, stat_s, stat_r, gain_s, gain_r, tot_s, tot_r,
):
    me = lax.axis_index("seq")
    row = lax.axis_index("dp")
    side = lax.rem(me, 2)
    partner = me + 1 - 2 * side
    up = lax.rem(me + 2, n_seq)
    down = lax.rem(me + n_seq - 2, n_seq)
    chunks = heads // GROUP

    def remote(src, dst, send, recv, device):
        return pltpu.make_async_remote_copy(
            src_ref=src, dst_ref=dst, send_sem=send, recv_sem=recv,
            device_id=device, device_id_type=pl.DeviceIdType.MESH,
        )

    def kv(c, src, dst, target):
        return remote(kvw.at[c, src], kvw.at[c, dst], kv_s.at[c, dst], kv_r.at[c, dst], {"seq": target})

    def qd(c, src, dst, target):
        return remote(qdw.at[c, src], qdw.at[c, dst], qd_s.at[c, dst], qd_r.at[c, dst], {"seq": target})

    def doc(o):
        target = lax.rem(me + o + n_seq, n_seq)
        s = REACH - o
        return remote(docw.at[REACH], docw.at[s], doc_s.at[s], doc_r.at[s], {"seq": target})

    def stat(c, t):
        target = lax.rem(me - t + n_seq, n_seq)
        return remote(statw.at[c, 0], statw.at[c, t], stat_s.at[c, t], stat_r.at[c, t], {"seq": target})

    def gain(h, source):
        return remote(gsend.at[h], grecv.at[source], gain_s.at[h], gain_r.at[source], {"seq": h})

    def total(p, source):
        return remote(tsend, trecv.at[source], tot_s.at[p], tot_r.at[source], {"dp": p})

    offsets = [o for o in range(-REACH, REACH + 1) if o != 0]

    barrier = pltpu.get_barrier_semaphore()

    def greet_seq(p, carry):
        @pl.when(p != me)
        def _():
            pl.semaphore_signal(barrier, inc=1, device_id={"seq": p}, device_id_type=pl.DeviceIdType.MESH)
        return carry

    def greet_dp(p, carry):
        @pl.when(p != row)
        def _():
            pl.semaphore_signal(barrier, inc=1, device_id={"dp": p}, device_id_type=pl.DeviceIdType.MESH)
        return carry

    lax.fori_loop(0, n_seq, greet_seq, 0)
    lax.fori_loop(0, n_dp, greet_dp, 0)
    docw[REACH] = jnp.broadcast_to(doc_ref[...].astype(jnp.float32), (8, BLOCK))
    pl.semaphore_wait(barrier, n_seq - 1 + n_dp - 1)
    for o in offsets:
        doc(o).start()

    def lanes(h):
        return pl.ds(pl.multiple_of(h * HD, HD), HD)

    def normed(ref, gains, h):
        x = ref[:, lanes(h)].astype(jnp.float32)
        return (x * inverse_rms(x) * gains[pl.ds(h, 1), :]).astype(jnp.bfloat16)

    def first(c):
        for g in range(GROUP):
            h = c * GROUP + g
            kvw[c, REACH, g, 0] = normed(k_ref, gk_ref, h)
            kvw[c, REACH, g, 1] = v_ref[:, lanes(h)]
            qdw[c, 0, g, 0] = normed(q_ref, gq_ref, h)
            qdw[c, 0, g, 1] = d_ref[:, lanes(h)]
        kv(c, 4, 2, up).start()
        qd(c, 0, 2, down).start()

        @pl.when(side == 0)
        def _():
            kv(c, 4, 3, partner).start()

        @pl.when(side == 1)
        def _():
            qd(c, 0, 1, partner).start()

    def forward(c):
        kv(c, 4, 2, up).wait_recv()
        kv(c, 2, 0, up).start()
        kv(c, 2, 1 + 2 * side, partner).start()
        qd(c, 0, 2, down).wait_recv()
        qd(c, 2, 4, down).start()
        qd(c, 2, 1 + 2 * side, partner).start()

    def across(c):
        kv(c, 2, 0, up).wait_recv()
        qd(c, 2, 4, down).wait_recv()

        @pl.when(side == 1)
        def _():
            kv(c, 0, 1, partner).start()

        @pl.when(side == 0)
        def _():
            qd(c, 4, 3, partner).start()

    def masks():
        for o in offsets:
            doc(o).wait_recv()
        own = jnp.broadcast_to(docw[REACH, 0:1, :], (BLOCK, BLOCK)).T
        rows = lax.broadcasted_iota(jnp.int32, (BLOCK, BLOCK), 0)
        cols = lax.broadcasted_iota(jnp.int32, (BLOCK, BLOCK), 1)
        for s in range(SLOTS):
            ids = jnp.where(me - REACH + s >= 0, docw[s, 0:1, :], -1.0)
            allowed = own == ids
            if s == REACH:
                allowed = allowed & (cols <= rows)
            bias_q[:, s * BLOCK:(s + 1) * BLOCK] = jnp.where(allowed, 0.0, MASKED)
        for t in range(SLOTS):
            ids = jnp.where(me + t < n_seq, docw[REACH + t, 0:1, :], -1.0)
            allowed = own == ids
            if t == 0:
                allowed = allowed & (rows <= cols)
            bias_k[:, t * BLOCK:(t + 1) * BLOCK] = jnp.where(allowed, 0.0, MASKED)

    def norm_back(ref, gains, h, grad):
        x = ref[:, lanes(h)].astype(jnp.float32)
        rec = inverse_rms(x)
        hat = x * rec
        scaled = grad * gains[pl.ds(h, 1), :]
        back = rec * (scaled - hat * jnp.mean(scaled * hat, axis=-1, keepdims=True))
        return back.astype(jnp.bfloat16), jnp.sum(grad * hat, axis=0, keepdims=True)

    def window(ref, c, g, i):
        return ref[c, :, g, i].reshape(SLOTS * BLOCK, HD)

    def queries(c):
        kv(c, 4, 3, partner).wait_recv()
        kv(c, 4, 1, partner).wait_recv()
        lane = lax.broadcasted_iota(jnp.int32, (BLOCK, BLOCK), 1)
        stats = jnp.zeros((BLOCK, BLOCK), jnp.float32)
        for g in range(GROUP):
            h = c * GROUP + g
            keys = window(kvw, c, g, 0)
            s = dot_nt(qdw[c, 0, g, 0], keys) * (SCALE * LOG2E) + bias_q[...]
            dprob = dot_nt(qdw[c, 0, g, 1], window(kvw, c, g, 1))
            peak = jnp.max(s, axis=1, keepdims=True)
            e = jnp.exp2(s - peak)
            weight = jnp.sum(e, axis=1, keepdims=True)
            inv = 1.0 / weight
            delta = jnp.sum(e * dprob, axis=1, keepdims=True) * inv
            dscore = (e * (inv * SCALE) * (dprob - delta)).astype(jnp.bfloat16)
            grad, term = norm_back(q_ref, gq_ref, h, dot_nn(dscore, keys))
            dq_out[:, lanes(h)] = grad
            gsend[h] = jnp.broadcast_to(term, (8, HD))
            stats = jnp.where(lane == 2 * g, peak + jnp.log2(weight), stats)
            stats = jnp.where(lane == 2 * g + 1, delta, stats)
        statw[c, 0] = stats.T[0:8]
        for t in range(1, SLOTS):
            stat(c, t).start()

    def keys_side(c):
        qd(c, 0, 1, partner).wait_recv()
        qd(c, 0, 3, partner).wait_recv()
        for t in range(1, SLOTS):
            stat(c, t).wait_recv()
        for g in range(GROUP):
            h = c * GROUP + g
            lse = jnp.concatenate([statw[c, t, 2 * g:2 * g + 1, :] for t in range(SLOTS)], axis=1)
            delta = jnp.concatenate([statw[c, t, 2 * g + 1:2 * g + 2, :] for t in range(SLOTS)], axis=1)
            qs = window(qdw, c, g, 0)
            ds = window(qdw, c, g, 1)
            s = dot_nt(kvw[c, REACH, g, 0], qs) * (SCALE * LOG2E) + bias_k[...]
            p = jnp.exp2(s - lse)
            dv_out[:, lanes(h)] = dot_nn(p.astype(jnp.bfloat16), ds).astype(jnp.bfloat16)
            dprob = dot_nt(kvw[c, REACH, g, 1], ds)
            dscore = (p * SCALE * (dprob - delta)).astype(jnp.bfloat16)
            grad, term = norm_back(k_ref, gk_ref, h, dot_nn(dscore, qs))
            dk_out[:, lanes(h)] = grad
            gsend[h, 1:2] = term

            @pl.when(h != me)
            def _():
                gain(h, me).start()

    def step(t, carry):
        @pl.when(t < chunks)
        def _():
            first(t)

        @pl.when((t >= FORWARD) & (t < chunks + FORWARD))
        def _():
            forward(t - FORWARD)

        @pl.when((t >= ACROSS) & (t < chunks + ACROSS))
        def _():
            across(t - ACROSS)

        @pl.when(t == QUERIES)
        def _():
            masks()

        @pl.when((t >= QUERIES) & (t < chunks + QUERIES))
        def _():
            queries(t - QUERIES)

        @pl.when((t >= KEYS) & (t < chunks + KEYS))
        def _():
            keys_side(t - KEYS)

        return carry

    lax.fori_loop(0, chunks + KEYS, step, 0)

    grecv[me] = gsend[me]

    def gain_wait(p, carry):
        @pl.when(p != me)
        def _():
            gain(me, p).wait_recv()
        return carry

    lax.fori_loop(0, n_seq, gain_wait, 0)
    tsend[...] = jnp.sum(grecv[...], axis=0)
    trecv[row] = tsend[...]

    def total_send(p, carry):
        @pl.when(p != row)
        def _():
            total(p, row).start()
        return carry

    lax.fori_loop(0, n_dp, total_send, 0)

    def drain(c, carry):
        for slot in range(REACH):
            kv(c, 4, slot, partner).wait_send()
            qd(c, 0, slot + 1, partner).wait_send()
            stat(c, slot + 1).wait_send()
        return carry

    lax.fori_loop(0, chunks, drain, 0)
    for o in offsets:
        doc(o).wait_send()

    def gain_drain(p, carry):
        @pl.when(p != me)
        def _():
            gain(p, me).wait_send()
        return carry

    lax.fori_loop(0, n_seq, gain_drain, 0)

    def total_wait(p, carry):
        @pl.when(p != row)
        def _():
            total(p, p).wait_recv()
            total(p, p).wait_send()
        return carry

    lax.fori_loop(0, n_dp, total_wait, 0)
    sums = jnp.sum(trecv[...], axis=0)
    gq_out[...] = sums[0:1]
    gk_out[...] = sums[1:2]


def body(query_states, key_states, value_states, out_grad, doc_ids, query_gain, key_gain):
    n_seq = lax.axis_size("seq")
    n_dp = lax.axis_size("dp")
    rows, feature = query_states.shape[1:]
    heads = feature // HD
    chunks = heads // GROUP
    window = (chunks, SLOTS, GROUP, 2, BLOCK, HD)
    dma = pltpu.SemaphoreType.DMA
    vmem = pl.BlockSpec(memory_space=pltpu.VMEM)
    grad = jax.ShapeDtypeStruct((rows, feature), jnp.bfloat16)
    gain = jax.ShapeDtypeStruct((1, HD), jnp.float32)
    pairs = heads * rows * SLOTS * BLOCK
    outs = pl.pallas_call(
        functools.partial(kernel, n_seq, n_dp, heads),
        out_shape=(grad, grad, grad, gain, gain),
        in_specs=[vmem] * 7,
        out_specs=(vmem,) * 5,
        scratch_shapes=[
            pltpu.VMEM(window, jnp.bfloat16),
            pltpu.VMEM(window, jnp.bfloat16),
            pltpu.VMEM((2 * REACH + 1, 8, BLOCK), jnp.float32),
            pltpu.VMEM((chunks, SLOTS, 8, BLOCK), jnp.float32),
            pltpu.VMEM((BLOCK, SLOTS * BLOCK), jnp.float32),
            pltpu.VMEM((BLOCK, SLOTS * BLOCK), jnp.float32),
            pltpu.VMEM((heads, 8, HD), jnp.float32),
            pltpu.VMEM((n_seq, 8, HD), jnp.float32),
            pltpu.VMEM((8, HD), jnp.float32),
            pltpu.VMEM((n_dp, 8, HD), jnp.float32),
            dma((chunks, SLOTS)), dma((chunks, SLOTS)),
            dma((chunks, SLOTS)), dma((chunks, SLOTS)),
            dma((2 * REACH + 1,)), dma((2 * REACH + 1,)),
            dma((chunks, SLOTS)), dma((chunks, SLOTS)),
            dma((heads,)), dma((n_seq,)),
            dma((n_dp,)), dma((n_dp,)),
        ],
        cost_estimate=pl.CostEstimate(
            flops=14 * pairs * HD, bytes_accessed=7 * rows * feature * 2, transcendentals=2 * pairs
        ),
        compiler_params=pltpu.CompilerParams(
            collective_id=0, has_side_effects=True, vmem_limit_bytes=40 * 1024 * 1024
        ),
    )(
        query_states[0], key_states[0], value_states[0], out_grad[0], doc_ids,
        query_gain.reshape(heads, HD), key_gain.reshape(heads, HD),
    )
    dq, dk, dv, gq, gk = outs
    return (dq[None], dk[None], dv[None], gq[0], gk[0])


def solution(mesh):
    split = P("dp", "seq", None)
    return jax.shard_map(
        body,
        mesh=mesh,
        in_specs=(split, split, split, split, P("dp", "seq"), P(), P()),
        out_specs=(split, split, split, P("seq"), P("seq")),
        check_vma=False,
    )
```

```python
import functools

import jax
import jax.numpy as jnp
from jax import lax
from jax.experimental import pallas as pl
from jax.experimental.pallas import tpu as pltpu
from jax.sharding import PartitionSpec as P

HD = 128
EPS = 1e-06
MASKED = -1e30
LOG2E = 1.4426950408889634
SCALE = HD ** (-0.5)

BLOCK = 128
PAIR = 2 * BLOCK
REACH = 2
SLOTS = REACH + 1
SPAN = 5 * BLOCK
MESH = pl.DeviceIdType.MESH
AHEAD, FORWARD, QUERIES, KEYS = 2, 1, 2, 3


def dot_nt(a, b):
    return lax.dot_general(a, b, (((1,), (1,)), ((), ())), preferred_element_type=jnp.float32)


def dot_nn(a, b):
    return lax.dot_general(a, b, (((1,), (0,)), ((), ())), preferred_element_type=jnp.float32)


def inverse_rms(x):
    return lax.rsqrt(jnp.mean(x * x, axis=-1, keepdims=True) + EPS)


def kernel(
    n_seq, n_dp, heads,
    q_ref, k_ref, v_ref, d_ref, doc_ref, gq_ref, gk_ref,
    dq_out, dk_out, dv_out, gq_out, gk_out,
    raw, kvw, qdw, outw, docw, statw, bias_q, bias_k, gsend, grecv, tsend, trecv,
    x_s, x_r, x_l, kv_s, kv_r, qd_s, qd_r, stat_s, stat_r, out_s, out_r, out_l,
    doc_s, doc_r, gain_s, gain_r, tot_s, tot_r,
):
    me = lax.axis_index("seq")
    row = lax.axis_index("dp")
    side = lax.rem(me, 2)
    level = me // 2
    levels = n_seq // 2
    partner = me + 1 - 2 * side
    chunks = heads // 2
    mine = pl.ds(pl.multiple_of(side * BLOCK, BLOCK), BLOCK)
    theirs = pl.ds(pl.multiple_of((1 - side) * BLOCK, BLOCK), BLOCK)

    def along(dz):
        return lax.rem(me + 2 * dz + n_seq, n_seq)

    def remote(src, dst, send, recv, device):
        return pltpu.make_async_remote_copy(
            src_ref=src, dst_ref=dst, send_sem=send, recv_sem=recv,
            device_id=device, device_id_type=MESH,
        )

    def lanes(h):
        return pl.ds(pl.multiple_of(h * HD, HD), HD)

    def head(c):
        return side * chunks + c

    def other(c):
        return (1 - side) * chunks + c

    sources = (q_ref, k_ref, v_ref, d_ref)
    results = (dq_out, dk_out, dv_out)

    def landing(c, a):
        if a < 2:
            return raw.at[c, a, mine]
        if a == 2:
            return kvw.at[c, REACH, 1, mine]
        return qdw.at[c, 0, 1, mine]

    def swap(c, a):
        return remote(
            sources[a].at[:, lanes(other(c))], landing(c, a), x_s.at[c, a], x_r.at[c, a], {"seq": partner}
        )

    def keep(c, a):
        return pltpu.make_async_copy(sources[a].at[:, lanes(head(c))], landing(c, a), x_l.at[c, a])

    def kv(c, dst):
        return remote(kvw.at[c, dst + 1], kvw.at[c, dst], kv_s.at[c, dst], kv_r.at[c, dst], {"seq": along(1)})

    def qd(c, dst):
        return remote(qdw.at[c, dst - 1], qdw.at[c, dst], qd_s.at[c, dst], qd_r.at[c, dst], {"seq": along(-1)})

    def stat(c, t):
        return remote(statw.at[c, 0], statw.at[c, t], stat_s.at[c, t], stat_r.at[c, t], {"seq": along(-t)})

    def give(c, a):
        return remote(
            outw.at[c, a, theirs], results[a].at[:, lanes(head(c))], out_s.at[c, a], out_r.at[c, a],
            {"seq": partner},
        )

    def put(c, a):
        return pltpu.make_async_copy(outw.at[c, a, mine], results[a].at[:, lanes(head(c))], out_l.at[c, a])

    near = [(dz, flip) for dz in range(-REACH, REACH + 1) for flip in (0, 1) if (dz, flip) != (0, 0)]

    def doc(dz, flip):
        there = side + flip - 2 * side * flip
        target = lax.rem(me - side + there + 2 * dz + n_seq, n_seq)
        slot = 2 * (REACH - dz) + side
        return remote(docw.at[2 * REACH + side], docw.at[slot], doc_s.at[2 * (dz + REACH) + flip],
                      doc_r.at[slot], {"seq": target})

    def doc_arrived(dz, flip):
        there = side + flip - 2 * side * flip
        slot = 2 * (REACH + dz) + there
        return remote(docw.at[slot], docw.at[slot], doc_s.at[slot], doc_r.at[slot], {"seq": partner})

    def gain(c, source):
        return remote(gsend.at[c], grecv.at[source], gain_s.at[c], gain_r.at[source], {"seq": head(c)})

    def total(p, source):
        return remote(tsend, trecv.at[source], tot_s.at[p], tot_r.at[source], {"dp": p})

    barrier = pltpu.get_barrier_semaphore()

    def greet_seq(p, carry):
        @pl.when(p != me)
        def _():
            pl.semaphore_signal(barrier, inc=1, device_id={"seq": p}, device_id_type=MESH)
        return carry

    def greet_dp(p, carry):
        @pl.when(p != row)
        def _():
            pl.semaphore_signal(barrier, inc=1, device_id={"dp": p}, device_id_type=MESH)
        return carry

    lax.fori_loop(0, n_seq, greet_seq, 0)
    lax.fori_loop(0, n_dp, greet_dp, 0)

    def keep_all(c, carry):
        for a in range(4):
            keep(c, a).start()
        return carry

    lax.fori_loop(0, chunks, keep_all, 0)
    docw[2 * REACH + side] = jnp.broadcast_to(doc_ref[...].astype(jnp.float32), (8, BLOCK))
    pl.semaphore_wait(barrier, n_seq - 1 + n_dp - 1)

    def swap_start(c):
        for a in (1, 2, 0, 3):
            swap(c, a).start()

    for c in range(AHEAD):
        swap_start(c)
    for dz, flip in near:
        doc(dz, flip).start()

    def normed(x, gains, h):
        x = x.astype(jnp.float32)
        return (x * inverse_rms(x) * gains[pl.ds(h, 1), :]).astype(jnp.bfloat16)

    def first(c):
        for a in range(4):
            keep(c, a).wait()
        for a in (1, 2):
            swap(c, a).wait_recv()
        kvw[c, REACH, 0] = normed(raw[c, 1], gk_ref, head(c))
        kv(c, 1).start()
        for a in (0, 3):
            swap(c, a).wait_recv()
        qdw[c, 0, 0] = normed(raw[c, 0], gq_ref, head(c))
        qd(c, 1).start()

    def forward(c):
        kv(c, 1).wait_recv()
        kv(c, 0).start()
        qd(c, 1).wait_recv()
        qd(c, 2).start()

    def masks():
        for dz, flip in near:
            doc_arrived(dz, flip).wait_recv()
        rows = lax.broadcasted_iota(jnp.int32, (BLOCK, BLOCK), 0)
        cols = lax.broadcasted_iota(jnp.int32, (BLOCK, BLOCK), 1)
        middle = 2 * REACH
        for sub in range(2):
            own = jnp.broadcast_to(docw[middle + sub, 0:1, :], (BLOCK, BLOCK)).T
            for j in range(5):
                slot = sub + j
                ids = jnp.where(level + slot // 2 - REACH >= 0, docw[slot, 0:1, :], -1.0)
                allowed = own == ids
                if slot == middle + sub:
                    allowed = allowed & (cols <= rows)
                bias_q[sub, :, j * BLOCK:(j + 1) * BLOCK] = jnp.where(allowed, 0.0, MASKED)
                slot = middle + sub + j
                ids = jnp.where(level + slot // 2 - REACH < levels, docw[slot, 0:1, :], -1.0)
                allowed = own == ids
                if j == 0:
                    allowed = allowed & (rows <= cols)
                bias_k[sub, :, j * BLOCK:(j + 1) * BLOCK] = jnp.where(allowed, 0.0, MASKED)

    def norm_back(x, gains, h, grad):
        x = x.astype(jnp.float32)
        rec = inverse_rms(x)
        hat = x * rec
        scaled = grad * gains[pl.ds(h, 1), :]
        back = rec * (scaled - hat * jnp.mean(scaled * hat, axis=-1, keepdims=True))
        return back.astype(jnp.bfloat16), jnp.sum(grad * hat, axis=0, keepdims=True)

    def window(ref, c, a, lo):
        return ref[c, :, a].reshape(SLOTS * PAIR, HD)[lo:lo + SPAN]

    def queries(c):
        kv(c, 0).wait_recv()
        lane = lax.broadcasted_iota(jnp.int32, (BLOCK, BLOCK), 1)
        terms = []
        for sub in range(2):
            lo = sub * BLOCK
            hi = lo + BLOCK
            keys = window(kvw, c, 0, lo)
            s = dot_nt(qdw[c, 0, 0, lo:hi], keys) * (SCALE * LOG2E) + bias_q[sub]
            dprob = dot_nt(qdw[c, 0, 1, lo:hi], window(kvw, c, 1, lo))
            peak = jnp.max(s, axis=1, keepdims=True)
            e = jnp.exp2(s - peak)
            weight = jnp.sum(e, axis=1, keepdims=True)
            inv = 1.0 / weight
            delta = jnp.sum(e * dprob, axis=1, keepdims=True) * inv
            dscore = (e * (inv * SCALE) * (dprob - delta)).astype(jnp.bfloat16)
            grad, term = norm_back(raw[c, 0, lo:hi], gq_ref, head(c), dot_nn(dscore, keys))
            outw[c, 0, lo:hi] = grad
            terms.append(term)
            stats = jnp.where(lane == 0, peak + jnp.log2(weight), delta)
            statw[c, 0, :, lo:hi] = stats.T[0:8]
        for t in range(1, SLOTS):
            stat(c, t).start()
        give(c, 0).start()
        put(c, 0).start()
        gsend[c] = jnp.broadcast_to(terms[0] + terms[1], (8, HD))

    def keys_side(c):
        qd(c, 2).wait_recv()
        for t in range(1, SLOTS):
            stat(c, t).wait_recv()
        lse = jnp.concatenate([statw[c, t, 0:1, :] for t in range(SLOTS)], axis=1)
        delta = jnp.concatenate([statw[c, t, 1:2, :] for t in range(SLOTS)], axis=1)
        terms = []
        for sub in range(2):
            lo = sub * BLOCK
            hi = lo + BLOCK
            qs = window(qdw, c, 0, lo)
            ds = window(qdw, c, 1, lo)
            s = dot_nt(kvw[c, REACH, 0, lo:hi], qs) * (SCALE * LOG2E) + bias_k[sub]
            p = jnp.exp2(s - lse[:, lo:lo + SPAN])
            outw[c, 2, lo:hi] = dot_nn(p.astype(jnp.bfloat16), ds).astype(jnp.bfloat16)
            dprob = dot_nt(kvw[c, REACH, 1, lo:hi], ds)
            dscore = (p * SCALE * (dprob - delta[:, lo:lo + SPAN])).astype(jnp.bfloat16)
            grad, term = norm_back(raw[c, 1, lo:hi], gk_ref, head(c), dot_nn(dscore, qs))
            outw[c, 1, lo:hi] = grad
            terms.append(term)
        gsend[c, 1:2] = terms[0] + terms[1]

        @pl.when(head(c) != me)
        def _():
            gain(c, level).start()

        for a in (1, 2):
            give(c, a).start()
            put(c, a).start()

    def step(t, carry):
        @pl.when(t + AHEAD < chunks)
        def _():
            swap_start(t + AHEAD)

        @pl.when(t < chunks)
        def _():
            first(t)

        @pl.when((t >= FORWARD) & (t < chunks + FORWARD))
        def _():
            forward(t - FORWARD)

        @pl.when(t == FORWARD)
        def _():
            masks()

        @pl.when((t >= QUERIES) & (t < chunks + QUERIES))
        def _():
            queries(t - QUERIES)

        @pl.when((t >= KEYS) & (t < chunks + KEYS))
        def _():
            keys_side(t - KEYS)

        return carry

    lax.fori_loop(0, chunks + KEYS, step, 0)

    owner = me // chunks

    @pl.when(owner == side)
    def _():
        grecv[level] = gsend[me - side * chunks]

    def gain_wait(z, carry):
        @pl.when(2 * z + owner != me)
        def _():
            gain(0, z).wait_recv()
        return carry

    lax.fori_loop(0, levels, gain_wait, 0)
    tsend[...] = jnp.sum(grecv[...], axis=0)
    trecv[row] = tsend[...]

    def total_send(p, carry):
        @pl.when(p != row)
        def _():
            total(p, row).start()
        return carry

    lax.fori_loop(0, n_dp, total_send, 0)

    def drain(c, carry):
        for a in range(4):
            swap(c, a).wait_send()
        for t in range(REACH):
            kv(c, t).wait_send()
            qd(c, t + 1).wait_send()
            stat(c, t + 1).wait_send()
        for a in range(3):
            give(c, a).wait()
            put(c, a).wait()

        @pl.when(head(c) != me)
        def _():
            gain(c, level).wait_send()
        return carry

    lax.fori_loop(0, chunks, drain, 0)
    for dz, flip in near:
        doc(dz, flip).wait_send()

    def total_wait(p, carry):
        @pl.when(p != row)
        def _():
            total(p, p).wait()
        return carry

    lax.fori_loop(0, n_dp, total_wait, 0)
    sums = jnp.sum(trecv[...], axis=0)
    gq_out[...] = sums[0:1]
    gk_out[...] = sums[1:2]


def body(query_states, key_states, value_states, out_grad, doc_ids, query_gain, key_gain):
    n_seq = lax.axis_size("seq")
    n_dp = lax.axis_size("dp")
    rows, feature = query_states.shape[1:]
    heads = feature // HD
    chunks = heads // 2
    window = (chunks, SLOTS, 2, PAIR, HD)
    dma = pltpu.SemaphoreType.DMA
    vmem = pl.BlockSpec(memory_space=pltpu.VMEM)
    anywhere = pl.BlockSpec(memory_space=pl.ANY)
    grad = jax.ShapeDtypeStruct((rows, feature), jnp.bfloat16)
    gain = jax.ShapeDtypeStruct((1, HD), jnp.float32)
    pairs = heads * rows * SPAN
    outs = pl.pallas_call(
        functools.partial(kernel, n_seq, n_dp, heads),
        out_shape=(grad, grad, grad, gain, gain),
        in_specs=[anywhere] * 4 + [vmem] * 3,
        out_specs=(anywhere,) * 3 + (vmem,) * 2,
        scratch_shapes=[
            pltpu.VMEM((chunks, 2, PAIR, HD), jnp.bfloat16),
            pltpu.VMEM(window, jnp.bfloat16),
            pltpu.VMEM(window, jnp.bfloat16),
            pltpu.VMEM((chunks, 3, PAIR, HD), jnp.bfloat16),
            pltpu.VMEM((4 * REACH + 2, 8, BLOCK), jnp.float32),
            pltpu.VMEM((chunks, SLOTS, 8, PAIR), jnp.float32),
            pltpu.VMEM((2, BLOCK, SPAN), jnp.float32),
            pltpu.VMEM((2, BLOCK, SPAN), jnp.float32),
            pltpu.VMEM((chunks, 8, HD), jnp.float32),
            pltpu.VMEM((n_seq // 2, 8, HD), jnp.float32),
            pltpu.VMEM((8, HD), jnp.float32),
            pltpu.VMEM((n_dp, 8, HD), jnp.float32),
            dma((chunks, 4)), dma((chunks, 4)), dma((chunks, 4)),
            dma((chunks, SLOTS)), dma((chunks, SLOTS)),
            dma((chunks, SLOTS)), dma((chunks, SLOTS)),
            dma((chunks, SLOTS)), dma((chunks, SLOTS)),
            dma((chunks, 3)), dma((chunks, 3)), dma((chunks, 3)),
            dma((4 * REACH + 2,)), dma((4 * REACH + 2,)),
            dma((chunks,)), dma((n_seq // 2,)),
            dma((n_dp,)), dma((n_dp,)),
        ],
        cost_estimate=pl.CostEstimate(
            flops=14 * pairs * HD, bytes_accessed=7 * rows * feature * 2, transcendentals=2 * pairs
        ),
        compiler_params=pltpu.CompilerParams(
            collective_id=0, has_side_effects=True, vmem_limit_bytes=60 * 1024 * 1024
        ),
    )(
        query_states[0], key_states[0], value_states[0], out_grad[0], doc_ids,
        query_gain.reshape(heads, HD), key_gain.reshape(heads, HD),
    )
    dq, dk, dv, gq, gk = outs
    return (dq[None], dk[None], dv[None], gq[0], gk[0])


def solution(mesh):
    split = P("dp", "seq", None)
    return jax.shard_map(
        body,
        mesh=mesh,
        in_specs=(split, split, split, split, P("dp", "seq"), P(), P()),
        out_specs=(split, split, split, P("seq"), P("seq")),
        check_vma=False,
    )
```

```python
import functools

import jax
import jax.numpy as jnp
from jax import lax
from jax.experimental import pallas as pl
from jax.experimental.pallas import tpu as pltpu
from jax.sharding import PartitionSpec as P

HD = 128
EPS = 1e-06
MASKED = -1e30
LOG2E = 1.4426950408889634
SCALE = HD ** (-0.5)

BLOCK = 128
PAIR = 2 * BLOCK
REACH = 2
SLOTS = REACH + 1
SPAN = 5 * BLOCK
MESH = pl.DeviceIdType.MESH
AHEAD, EARLY, FORWARD, QUERIES, KEYS = 4, 4, 2, 3, 5


def dot_nt(a, b):
    return lax.dot_general(a, b, (((1,), (1,)), ((), ())), preferred_element_type=jnp.float32)


def dot_nn(a, b):
    return lax.dot_general(a, b, (((1,), (0,)), ((), ())), preferred_element_type=jnp.float32)


def inverse_rms(x):
    return lax.rsqrt(jnp.mean(x * x, axis=-1, keepdims=True) + EPS)


def kernel(
    n_seq, n_dp, heads,
    q_ref, k_ref, v_ref, d_ref, doc_any, gq_any, gk_any,
    dq_out, dk_out, dv_out, gq_out, gk_out,
    gq_ref, gk_ref, doc_ref, raw, kvw, qdw, outw, docw, statw, bias_q, bias_k, gsend, grecv, tsend, trecv,
    x_s, x_r, x_l, kv_s, kv_r, qd_s, qd_r, stat_s, stat_r, out_s, out_r, out_l,
    doc_s, doc_r, gain_s, gain_r, tot_s, tot_r, small_s,
):
    me = lax.axis_index("seq")
    row = lax.axis_index("dp")
    side = lax.rem(me, 2)
    level = me // 2
    levels = n_seq // 2
    partner = me + 1 - 2 * side
    chunks = heads // 2
    mine = pl.ds(pl.multiple_of(side * BLOCK, BLOCK), BLOCK)
    theirs = pl.ds(pl.multiple_of((1 - side) * BLOCK, BLOCK), BLOCK)

    def along(dz):
        return lax.rem(me + 2 * dz + n_seq, n_seq)

    def remote(src, dst, send, recv, device):
        return pltpu.make_async_remote_copy(
            src_ref=src, dst_ref=dst, send_sem=send, recv_sem=recv,
            device_id=device, device_id_type=MESH,
        )

    def lanes(h):
        return pl.ds(pl.multiple_of(h * HD, HD), HD)

    def head(c):
        return side * chunks + c

    def other(c):
        return (1 - side) * chunks + c

    sources = (q_ref, k_ref, v_ref, d_ref)
    results = (dq_out, dk_out, dv_out)

    def landing(c, a):
        if a < 2:
            return raw.at[c, a, mine]
        if a == 2:
            return kvw.at[c, REACH, 1, mine]
        return qdw.at[c, 0, 1, mine]

    def swap(c, a):
        return remote(
            sources[a].at[:, lanes(other(c))], landing(c, a), x_s.at[c, a], x_r.at[c, a], {"seq": partner}
        )

    def keep(c, a):
        return pltpu.make_async_copy(sources[a].at[:, lanes(head(c))], landing(c, a), x_l.at[c, a])

    def kv(c):
        return remote(kvw.at[c, 1], kvw.at[c, 0], kv_s.at[c, 2], kv_r.at[c, 2], {"seq": along(1)})

    def qd(c):
        return remote(qdw.at[c, 1], qdw.at[c, 2], qd_s.at[c, 2], qd_r.at[c, 2], {"seq": along(-1)})

    def kv_half(c, i):
        half = (mine, theirs)[i]
        return remote(kvw.at[c, 2, :, half], kvw.at[c, 1, :, half], kv_s.at[c, i], kv_r.at[c, i], {"seq": along(1)})

    def qd_half(c, i):
        half = (mine, theirs)[i]
        return remote(qdw.at[c, 0, :, half], qdw.at[c, 1, :, half], qd_s.at[c, i], qd_r.at[c, i], {"seq": along(-1)})

    def stat(c, t):
        return remote(statw.at[c, 0], statw.at[c, t], stat_s.at[c, t], stat_r.at[c, t], {"seq": along(-t)})

    def give(c, a):
        return remote(
            outw.at[c, a, theirs], results[a].at[:, lanes(head(c))], out_s.at[c, a], out_r.at[c, a],
            {"seq": partner},
        )

    def put(c, a):
        return pltpu.make_async_copy(outw.at[c, a, mine], results[a].at[:, lanes(head(c))], out_l.at[c, a])

    near = [(dz, flip) for dz in range(-REACH, REACH + 1) for flip in (0, 1) if (dz, flip) != (0, 0)]

    def doc(dz, flip):
        there = side + flip - 2 * side * flip
        target = lax.rem(me - side + there + 2 * dz + n_seq, n_seq)
        slot = 2 * (REACH - dz) + side
        return remote(docw.at[2 * REACH + side], docw.at[slot], doc_s.at[2 * (dz + REACH) + flip],
                      doc_r.at[slot], {"seq": target})

    def doc_arrived(dz, flip):
        there = side + flip - 2 * side * flip
        slot = 2 * (REACH + dz) + there
        return remote(docw.at[slot], docw.at[slot], doc_s.at[slot], doc_r.at[slot], {"seq": partner})

    def gain(c, source):
        return remote(gsend.at[c], grecv.at[source], gain_s.at[c], gain_r.at[source], {"seq": head(c)})

    def total(p, source):
        return remote(tsend, trecv.at[source], tot_s.at[p], tot_r.at[source], {"dp": p})

    barrier = pltpu.get_barrier_semaphore()

    for o in range(1, n_seq):
        pl.semaphore_signal(barrier, inc=1, device_id={"seq": lax.rem(me + o, n_seq)}, device_id_type=MESH)
    for o in range(1, n_dp):
        pl.semaphore_signal(barrier, inc=1, device_id={"dp": lax.rem(row + o, n_dp)}, device_id_type=MESH)
    small = [
        pltpu.make_async_copy(src, dst, small_s.at[i])
        for i, (src, dst) in enumerate(((gq_any, gq_ref), (gk_any, gk_ref), (doc_any, doc_ref)))
    ]
    for copy in small:
        copy.start()

    def keep_all(c, carry):
        for a in range(4):
            keep(c, a).start()
        return carry

    def normed(x, gains, h):
        x = x.astype(jnp.float32)
        return (x * inverse_rms(x) * gains[pl.ds(h, 1), :]).astype(jnp.bfloat16)

    def norm_half(c, half):
        kvw[c, REACH, 0, half] = normed(raw[c, 1, half], gk_ref, head(c))
        qdw[c, 0, 0, half] = normed(raw[c, 0, half], gq_ref, head(c))

    def mine_ready(c):
        for a in range(4):
            keep(c, a).wait()
        norm_half(c, mine)

    def send_half(c, i):
        kv_half(c, i).start()
        qd_half(c, i).start()

    def swap_start(c):
        for a in (1, 2, 0, 3):
            swap(c, a).start()

    lax.fori_loop(0, chunks, keep_all, 0)
    for copy in small:
        copy.wait()
    docw[2 * REACH + side] = jnp.broadcast_to(doc_ref[...].astype(jnp.float32), (8, BLOCK))
    for c in range(EARLY):
        mine_ready(c)
    pl.semaphore_wait(barrier, n_seq - 1 + n_dp - 1)
    for c in range(AHEAD):
        swap_start(c)
    for c in range(EARLY):
        send_half(c, 0)
    for dz, flip in near:
        doc(dz, flip).start()

    def rest(c):
        for a in range(4):
            swap(c, a).wait_recv()
        norm_half(c, theirs)
        send_half(c, 1)

    def forward(c):
        for i in range(2):
            kv_half(c, i).wait_recv()
        kv(c).start()
        for i in range(2):
            qd_half(c, i).wait_recv()
        qd(c).start()

    def masks():
        for dz, flip in near:
            doc_arrived(dz, flip).wait_recv()
            doc(dz, flip).wait_send()
        rows = lax.broadcasted_iota(jnp.int32, (BLOCK, BLOCK), 0)
        cols = lax.broadcasted_iota(jnp.int32, (BLOCK, BLOCK), 1)
        middle = 2 * REACH
        for sub in range(2):
            own = jnp.broadcast_to(docw[middle + sub, 0:1, :], (BLOCK, BLOCK)).T
            for j in range(5):
                slot = sub + j
                ids = jnp.where(level + slot // 2 - REACH >= 0, docw[slot, 0:1, :], -1.0)
                allowed = own == ids
                if slot == middle + sub:
                    allowed = allowed & (cols <= rows)
                bias_q[sub, :, j * BLOCK:(j + 1) * BLOCK] = jnp.where(allowed, 0.0, MASKED)
                slot = middle + sub + j
                ids = jnp.where(level + slot // 2 - REACH < levels, docw[slot, 0:1, :], -1.0)
                allowed = own == ids
                if j == 0:
                    allowed = allowed & (rows <= cols)
                bias_k[sub, :, j * BLOCK:(j + 1) * BLOCK] = jnp.where(allowed, 0.0, MASKED)

    def norm_back(x, gains, h, grad):
        x = x.astype(jnp.float32)
        rec = inverse_rms(x)
        hat = x * rec
        scaled = grad * gains[pl.ds(h, 1), :]
        back = rec * (scaled - hat * jnp.mean(scaled * hat, axis=-1, keepdims=True))
        return back.astype(jnp.bfloat16), jnp.sum(grad * hat, axis=0, keepdims=True)

    def window(ref, c, a, lo):
        return ref[c, :, a].reshape(SLOTS * PAIR, HD)[lo:lo + SPAN]

    def queries(c):
        kv(c).wait_recv()
        lane = lax.broadcasted_iota(jnp.int32, (BLOCK, BLOCK), 1)
        terms = []
        for sub in range(2):
            lo = sub * BLOCK
            hi = lo + BLOCK
            keys = window(kvw, c, 0, lo)
            s = dot_nt(qdw[c, 0, 0, lo:hi], keys) * (SCALE * LOG2E) + bias_q[sub]
            dprob = dot_nt(qdw[c, 0, 1, lo:hi], window(kvw, c, 1, lo))
            peak = jnp.max(s, axis=1, keepdims=True)
            e = jnp.exp2(s - peak)
            weight = jnp.sum(e, axis=1, keepdims=True)
            inv = 1.0 / weight
            delta = jnp.sum(e * dprob, axis=1, keepdims=True) * inv
            dscore = (e * (inv * SCALE) * (dprob - delta)).astype(jnp.bfloat16)
            grad, term = norm_back(raw[c, 0, lo:hi], gq_ref, head(c), dot_nn(dscore, keys))
            outw[c, 0, lo:hi] = grad
            terms.append(term)
            stats = jnp.where(lane == 0, peak + jnp.log2(weight), delta)
            statw[c, 0, :, lo:hi] = stats.T[0:8]
        for t in range(1, SLOTS):
            stat(c, t).start()
        give(c, 0).start()
        put(c, 0).start()
        gsend[c] = jnp.broadcast_to(terms[0] + terms[1], (8, HD))

    def keys_side(c):
        qd(c).wait_recv()
        for t in range(1, SLOTS):
            stat(c, t).wait_recv()
        lse = jnp.concatenate([statw[c, t, 0:1, :] for t in range(SLOTS)], axis=1)
        delta = jnp.concatenate([statw[c, t, 1:2, :] for t in range(SLOTS)], axis=1)
        terms = []
        for sub in range(2):
            lo = sub * BLOCK
            hi = lo + BLOCK
            qs = window(qdw, c, 0, lo)
            ds = window(qdw, c, 1, lo)
            s = dot_nt(kvw[c, REACH, 0, lo:hi], qs) * (SCALE * LOG2E) + bias_k[sub]
            p = jnp.exp2(s - lse[:, lo:lo + SPAN])
            outw[c, 2, lo:hi] = dot_nn(p.astype(jnp.bfloat16), ds).astype(jnp.bfloat16)
            dprob = dot_nt(kvw[c, REACH, 1, lo:hi], ds)
            dscore = (p * SCALE * (dprob - delta[:, lo:lo + SPAN])).astype(jnp.bfloat16)
            grad, term = norm_back(raw[c, 1, lo:hi], gk_ref, head(c), dot_nn(dscore, qs))
            outw[c, 1, lo:hi] = grad
            terms.append(term)
        gsend[c, 1:2] = terms[0] + terms[1]

        @pl.when(head(c) != me)
        def _():
            gain(c, level).start()

        for a in (1, 2):
            give(c, a).start()
            put(c, a).start()

    def sent_early(c):
        for a in range(4):
            swap(c, a).wait_send()
        for i in range(2):
            kv_half(c, i).wait_send()
            qd_half(c, i).wait_send()
        kv(c).wait_send()
        qd(c).wait_send()
        stat(c, 1).wait_send()
        stat(c, 2).wait_send()
        give(c, 0).wait()
        put(c, 0).wait()

    def sent_late(c):
        for a in (1, 2):
            give(c, a).wait()
            put(c, a).wait()

        @pl.when(head(c) != me)
        def _():
            gain(c, level).wait_send()

    def step(t, carry):
        @pl.when(t + AHEAD < chunks)
        def _():
            swap_start(t + AHEAD)

        @pl.when(t < chunks)
        def _():
            rest(t)

        @pl.when(t + EARLY < chunks)
        def _():
            mine_ready(t + EARLY)
            send_half(t + EARLY, 0)

        @pl.when((t >= FORWARD) & (t < chunks + FORWARD))
        def _():
            forward(t - FORWARD)

        @pl.when(t == FORWARD)
        def _():
            masks()

        @pl.when((t >= KEYS) & (t < chunks + KEYS))
        def _():
            keys_side(t - KEYS)

        @pl.when((t >= QUERIES) & (t < chunks + QUERIES))
        def _():
            queries(t - QUERIES)

        @pl.when((t > KEYS) & (t < chunks + KEYS))
        def _():
            sent_early(t - KEYS - 1)
            sent_late(t - KEYS - 1)

        return carry

    lax.fori_loop(0, chunks + KEYS, step, 0)

    owner = me // chunks

    @pl.when(owner == side)
    def _():
        grecv[level] = gsend[me - side * chunks]

    def gain_wait(z, carry):
        @pl.when(2 * z + owner != me)
        def _():
            gain(0, z).wait_recv()
        return carry

    lax.fori_loop(0, levels, gain_wait, 0)
    tsend[...] = jnp.sum(grecv[...], axis=0)
    trecv[row] = tsend[...]

    def total_send(p, carry):
        @pl.when(p != row)
        def _():
            total(p, row).start()
        return carry

    lax.fori_loop(0, n_dp, total_send, 0)

    for c in range(chunks - 1, chunks):
        sent_early(c)
        sent_late(c)
    def total_wait(p, carry):
        @pl.when(p != row)
        def _():
            total(p, p).wait()
        return carry

    lax.fori_loop(0, n_dp, total_wait, 0)
    sums = jnp.sum(trecv[...], axis=0)
    gq_out[...] = sums[0:1]
    gk_out[...] = sums[1:2]


def hand_over(arrays):
    n = len(arrays)

    def move(*refs):
        sources, targets, rooms, sems = refs[:n], refs[n:2 * n], refs[2 * n:3 * n], refs[3 * n]
        loads = [pltpu.make_async_copy(sources[i], rooms[i], sems.at[0, i]) for i in range(n)]
        stores = [pltpu.make_async_copy(rooms[i], targets[i], sems.at[1, i]) for i in range(n)]
        for load in loads:
            load.start()
        for load, store in zip(loads, stores):
            load.wait()
            store.start()
        for store in stores:
            store.wait()

    anywhere = pl.BlockSpec(memory_space=pl.ANY)
    return pl.pallas_call(
        move,
        out_shape=tuple(jax.ShapeDtypeStruct(a.shape, a.dtype) for a in arrays),
        in_specs=[anywhere] * n,
        out_specs=(anywhere,) * n,
        scratch_shapes=[pltpu.VMEM(a.shape, a.dtype) for a in arrays] + [pltpu.SemaphoreType.DMA((2, n))],
        compiler_params=pltpu.CompilerParams(vmem_limit_bytes=60 * 1024 * 1024),
    )(*arrays)


def body(query_states, key_states, value_states, out_grad, doc_ids, query_gain, key_gain):
    n_seq = lax.axis_size("seq")
    n_dp = lax.axis_size("dp")
    rows, feature = query_states.shape[1:]
    heads = feature // HD
    chunks = heads // 2
    window = (chunks, SLOTS, 2, PAIR, HD)
    dma = pltpu.SemaphoreType.DMA
    vmem = pl.BlockSpec(memory_space=pltpu.VMEM)
    anywhere = pl.BlockSpec(memory_space=pl.ANY)
    grad = jax.ShapeDtypeStruct((rows, feature), jnp.bfloat16)
    gain = jax.ShapeDtypeStruct((1, HD), jnp.float32)
    pairs = heads * rows * SPAN
    outs = pl.pallas_call(
        functools.partial(kernel, n_seq, n_dp, heads),
        out_shape=(grad, grad, grad, gain, gain),
        in_specs=[anywhere] * 7,
        out_specs=(anywhere,) * 3 + (vmem,) * 2,
        scratch_shapes=[
            pltpu.VMEM((heads, HD), jnp.float32),
            pltpu.VMEM((heads, HD), jnp.float32),
            pltpu.VMEM((1, BLOCK), jnp.int32),
            pltpu.VMEM((chunks, 2, PAIR, HD), jnp.bfloat16),
            pltpu.VMEM(window, jnp.bfloat16),
            pltpu.VMEM(window, jnp.bfloat16),
            pltpu.VMEM((chunks, 3, PAIR, HD), jnp.bfloat16),
            pltpu.VMEM((4 * REACH + 2, 8, BLOCK), jnp.float32),
            pltpu.VMEM((chunks, SLOTS, 8, PAIR), jnp.float32),
            pltpu.VMEM((2, BLOCK, SPAN), jnp.float32),
            pltpu.VMEM((2, BLOCK, SPAN), jnp.float32),
            pltpu.VMEM((chunks, 8, HD), jnp.float32),
            pltpu.VMEM((n_seq // 2, 8, HD), jnp.float32),
            pltpu.VMEM((8, HD), jnp.float32),
            pltpu.VMEM((n_dp, 8, HD), jnp.float32),
            dma((chunks, 4)), dma((chunks, 4)), dma((chunks, 4)),
            dma((chunks, SLOTS)), dma((chunks, SLOTS)),
            dma((chunks, SLOTS)), dma((chunks, SLOTS)),
            dma((chunks, SLOTS)), dma((chunks, SLOTS)),
            dma((chunks, 3)), dma((chunks, 3)), dma((chunks, 3)),
            dma((4 * REACH + 2,)), dma((4 * REACH + 2,)),
            dma((chunks,)), dma((n_seq // 2,)),
            dma((n_dp,)), dma((n_dp,)), dma((3,)),
        ],
        cost_estimate=pl.CostEstimate(
            flops=14 * pairs * HD, bytes_accessed=7 * rows * feature * 2, transcendentals=2 * pairs
        ),
        compiler_params=pltpu.CompilerParams(
            collective_id=0, has_side_effects=True, vmem_limit_bytes=60 * 1024 * 1024
        ),
    )(
        query_states[0], key_states[0], value_states[0], out_grad[0], doc_ids,
        query_gain.reshape(heads, HD), key_gain.reshape(heads, HD),
    )
    dq, dk, dv, gq, gk = hand_over(outs)
    return (dq[None], dk[None], dv[None], gq[0], gk[0])


def solution(mesh):
    split = P("dp", "seq", None)
    return jax.shard_map(
        body,
        mesh=mesh,
        in_specs=(split, split, split, split, P("dp", "seq"), P(), P()),
        out_specs=(split, split, split, P("seq"), P("seq")),
        check_vma=False,
    )
```

```python
import functools

import jax
import jax.numpy as jnp
from jax import lax
from jax.experimental import pallas as pl
from jax.experimental.pallas import tpu as pltpu
from jax.sharding import PartitionSpec as P

HD = 128
EPS = 1e-06
MASKED = -1e30
LOG2E = 1.4426950408889634
SCALE = HD ** (-0.5)

BLOCK = 128
PAIR = 2 * BLOCK
REACH = 2
SLOTS = REACH + 1
SPAN = 5 * BLOCK
MESH = pl.DeviceIdType.MESH
AHEAD, EARLY, FORWARD, QUERIES, KEYS = 4, 4, 2, 3, 5


def dot_nt(a, b):
    return lax.dot_general(a, b, (((1,), (1,)), ((), ())), preferred_element_type=jnp.float32)


def dot_nn(a, b):
    return lax.dot_general(a, b, (((1,), (0,)), ((), ())), preferred_element_type=jnp.float32)


def inverse_rms(x):
    return lax.rsqrt(jnp.mean(x * x, axis=-1, keepdims=True) + EPS)


def kernel(
    n_seq, n_dp, heads,
    q_ref, k_ref, v_ref, d_ref, doc_any, gq_any, gk_any,
    dq_out, dk_out, dv_out, gq_out, gk_out,
    gq_ref, gk_ref, doc_ref, raw, kvw, qdw, outw, docw, statw, bias_q, bias_k, gsend, grecv, tsend, trecv,
    x_s, x_r, x_l, kv_s, kv_r, qd_s, qd_r, stat_s, stat_r, out_s, out_r, out_l,
    doc_s, doc_r, gain_s, gain_r, tot_s, tot_r, small_s,
):
    me = lax.axis_index("seq")
    row = lax.axis_index("dp")
    side = lax.rem(me, 2)
    level = me // 2
    levels = n_seq // 2
    partner = me + 1 - 2 * side
    chunks = heads // 2
    mine, theirs = side, 1 - side

    def along(dz):
        return lax.rem(me + 2 * dz + n_seq, n_seq)

    def remote(src, dst, send, recv, device):
        return pltpu.make_async_remote_copy(
            src_ref=src, dst_ref=dst, send_sem=send, recv_sem=recv,
            device_id=device, device_id_type=MESH,
        )

    def lanes(h):
        return pl.ds(pl.multiple_of(h * HD, HD), HD)

    def head(c):
        return side * chunks + c

    def other(c):
        return (1 - side) * chunks + c

    sources = (q_ref, k_ref, v_ref, d_ref)
    results = (dq_out, dk_out, dv_out)

    def landing(c, a):
        if a < 2:
            return raw.at[c, side, a]
        if a == 2:
            return kvw.at[c, REACH, side, 1]
        return qdw.at[c, 0, side, 1]

    def swap(c, a):
        return remote(
            sources[a].at[:, lanes(other(c))], landing(c, a), x_s.at[c, a], x_r.at[c, a], {"seq": partner}
        )

    def keep(c, a):
        return pltpu.make_async_copy(sources[a].at[:, lanes(head(c))], landing(c, a), x_l.at[c, a])

    def kv(c):
        return remote(kvw.at[c, 1], kvw.at[c, 0], kv_s.at[c, 2], kv_r.at[c, 2], {"seq": along(1)})

    def qd(c):
        return remote(qdw.at[c, 1], qdw.at[c, 2], qd_s.at[c, 2], qd_r.at[c, 2], {"seq": along(-1)})

    def kv_half(c, i):
        half = (mine, theirs)[i]
        return remote(kvw.at[c, 2, half], kvw.at[c, 1, half], kv_s.at[c, i], kv_r.at[c, i], {"seq": along(1)})

    def qd_half(c, i):
        half = (mine, theirs)[i]
        return remote(qdw.at[c, 0, half], qdw.at[c, 1, half], qd_s.at[c, i], qd_r.at[c, i], {"seq": along(-1)})

    def own(c, act):
        for i in range(2):
            act(kv_half(c, i))
            act(qd_half(c, i))

    def stat(c, t):
        return remote(statw.at[c, 0], statw.at[c, t], stat_s.at[c, t], stat_r.at[c, t], {"seq": along(-t)})

    def give(c, a):
        return remote(
            outw.at[c, a, theirs], results[a].at[:, lanes(head(c))], out_s.at[c, a], out_r.at[c, a],
            {"seq": partner},
        )

    def put(c, a):
        return pltpu.make_async_copy(outw.at[c, a, mine], results[a].at[:, lanes(head(c))], out_l.at[c, a])

    near = [(dz, flip) for dz in range(-REACH, REACH + 1) for flip in (0, 1) if (dz, flip) != (0, 0)]

    def doc(dz, flip):
        there = side + flip - 2 * side * flip
        target = lax.rem(me - side + there + 2 * dz + n_seq, n_seq)
        slot = 2 * (REACH - dz) + side
        return remote(docw.at[2 * REACH + side], docw.at[slot], doc_s.at[2 * (dz + REACH) + flip],
                      doc_r.at[slot], {"seq": target})

    def doc_arrived(dz, flip):
        there = side + flip - 2 * side * flip
        slot = 2 * (REACH + dz) + there
        return remote(docw.at[slot], docw.at[slot], doc_s.at[slot], doc_r.at[slot], {"seq": partner})

    def gain(c, source):
        return remote(gsend.at[c], grecv.at[source], gain_s.at[c], gain_r.at[source], {"seq": head(c)})

    def total(p, source):
        return remote(tsend, trecv.at[source], tot_s.at[p], tot_r.at[source], {"dp": p})

    barrier = pltpu.get_barrier_semaphore()

    for o in range(1, n_seq):
        pl.semaphore_signal(barrier, inc=1, device_id={"seq": lax.rem(me + o, n_seq)}, device_id_type=MESH)
    for o in range(1, n_dp):
        pl.semaphore_signal(barrier, inc=1, device_id={"dp": lax.rem(row + o, n_dp)}, device_id_type=MESH)
    small = [
        pltpu.make_async_copy(src, dst, small_s.at[i])
        for i, (src, dst) in enumerate(((gq_any, gq_ref), (gk_any, gk_ref), (doc_any, doc_ref)))
    ]
    for copy in small:
        copy.start()

    def keep_all(c, carry):
        for a in range(4):
            keep(c, a).start()
        return carry

    def normed(x, gains, h):
        x = x.astype(jnp.float32)
        return (x * inverse_rms(x) * gains[pl.ds(h, 1), :]).astype(jnp.bfloat16)

    def norm_half(c, half):
        kvw[c, REACH, half, 0] = normed(raw[c, half, 1], gk_ref, head(c))
        qdw[c, 0, half, 0] = normed(raw[c, half, 0], gq_ref, head(c))

    def mine_ready(c):
        for a in range(4):
            keep(c, a).wait()
        norm_half(c, mine)

    def send_half(c, i):
        kv_half(c, i).start()
        qd_half(c, i).start()

    def swap_start(c):
        for a in (1, 2, 0, 3):
            swap(c, a).start()

    lax.fori_loop(0, chunks, keep_all, 0)
    for copy in small:
        copy.wait()
    docw[2 * REACH + side] = jnp.broadcast_to(doc_ref[...].astype(jnp.float32), (8, BLOCK))
    for c in range(EARLY):
        mine_ready(c)
    pl.semaphore_wait(barrier, n_seq - 1 + n_dp - 1)
    for c in range(AHEAD):
        swap_start(c)
    for c in range(EARLY):
        send_half(c, 0)
    for dz, flip in near:
        doc(dz, flip).start()

    def rest(c):
        for a in range(4):
            swap(c, a).wait_recv()
        norm_half(c, theirs)
        send_half(c, 1)

    def forward(c):
        own(c, lambda copy: copy.wait_recv())
        kv(c).start()
        qd(c).start()

    def masks():
        for dz, flip in near:
            doc_arrived(dz, flip).wait_recv()
            doc(dz, flip).wait_send()
        rows = lax.broadcasted_iota(jnp.int32, (BLOCK, BLOCK), 0)
        cols = lax.broadcasted_iota(jnp.int32, (BLOCK, BLOCK), 1)
        middle = 2 * REACH
        for sub in range(2):
            own = jnp.broadcast_to(docw[middle + sub, 0:1, :], (BLOCK, BLOCK)).T
            for j in range(5):
                slot = sub + j
                ids = jnp.where(level + slot // 2 - REACH >= 0, docw[slot, 0:1, :], -1.0)
                allowed = own == ids
                if slot == middle + sub:
                    allowed = allowed & (cols <= rows)
                bias_q[sub, :, j * BLOCK:(j + 1) * BLOCK] = jnp.where(allowed, 0.0, MASKED)
                slot = middle + sub + j
                ids = jnp.where(level + slot // 2 - REACH < levels, docw[slot, 0:1, :], -1.0)
                allowed = own == ids
                if j == 0:
                    allowed = allowed & (rows <= cols)
                bias_k[sub, :, j * BLOCK:(j + 1) * BLOCK] = jnp.where(allowed, 0.0, MASKED)

    def norm_back(x, gains, h, grad):
        x = x.astype(jnp.float32)
        rec = inverse_rms(x)
        hat = x * rec
        scaled = grad * gains[pl.ds(h, 1), :]
        back = rec * (scaled - hat * jnp.mean(scaled * hat, axis=-1, keepdims=True))
        return back.astype(jnp.bfloat16), jnp.sum(grad * hat, axis=0, keepdims=True)

    def window(ref, c, a, sub):
        parts = [ref[c, (sub + j) // 2, lax.rem(sub + j, 2), a] for j in range(5)]
        return jnp.concatenate(parts, axis=0)

    def queries(c):
        kv(c).wait_recv()
        lane = lax.broadcasted_iota(jnp.int32, (BLOCK, BLOCK), 1)
        terms, key_terms = [], []
        for sub in range(2):
            lo = sub * BLOCK
            hi = lo + BLOCK
            keys = window(kvw, c, 0, sub)
            s = dot_nt(qdw[c, 0, sub, 0], keys) * (SCALE * LOG2E) + bias_q[sub]
            dprob = dot_nt(qdw[c, 0, sub, 1], window(kvw, c, 1, sub))
            peak = jnp.max(s, axis=1, keepdims=True)
            e = jnp.exp2(s - peak)
            weight = jnp.sum(e, axis=1, keepdims=True)
            inv = 1.0 / weight
            delta = jnp.sum(e * dprob, axis=1, keepdims=True) * inv
            dscore = (e * (inv * SCALE) * (dprob - delta)).astype(jnp.bfloat16)
            grad = dot_nn(dscore, keys)
            back, term = norm_back(raw[c, sub, 0], gq_ref, head(c), grad)
            outw[c, 0, sub] = back
            terms.append(term)
            key_terms.append(jnp.sum(grad * qdw[c, 0, sub, 0].astype(jnp.float32), axis=0, keepdims=True))
            stats = jnp.where(lane == 0, peak + jnp.log2(weight), delta)
            statw[c, 0, :, lo:hi] = stats.T[0:8]
        for t in range(1, SLOTS):
            stat(c, t).start()
        sublane = lax.broadcasted_iota(jnp.int32, (8, HD), 0)
        gsend[c] = jnp.where(sublane == 0, terms[0] + terms[1], key_terms[0] + key_terms[1])

        @pl.when(head(c) != me)
        def _():
            gain(c, level).start()

        give(c, 0).start()
        put(c, 0).start()

    def keys_side(c):
        qd(c).wait_recv()
        for t in range(1, SLOTS):
            stat(c, t).wait_recv()
        def stat_row(r, sub):
            parts = [
                statw[c, (sub + j) // 2, r:r + 1, pl.ds(pl.multiple_of(lax.rem(sub + j, 2) * BLOCK, BLOCK), BLOCK)]
                for j in range(5)
            ]
            return jnp.concatenate(parts, axis=1)

        for i, sub in enumerate((theirs, mine)):
            qs = window(qdw, c, 0, sub)
            ds = window(qdw, c, 1, sub)
            s = dot_nt(kvw[c, REACH, sub, 0], qs) * (SCALE * LOG2E) + bias_k[sub]
            p = jnp.exp2(s - stat_row(0, sub))
            outw[c, 2, sub] = dot_nn(p.astype(jnp.bfloat16), ds).astype(jnp.bfloat16)
            dprob = dot_nt(kvw[c, REACH, sub, 1], ds)
            dscore = (p * SCALE * (dprob - stat_row(1, sub))).astype(jnp.bfloat16)
            outw[c, 1, sub], _ = norm_back(raw[c, sub, 1], gk_ref, head(c), dot_nn(dscore, qs))
            if i == 0:
                for a in (1, 2):
                    give(c, a).start()
        for a in (1, 2):
            put(c, a).start()

    def sent_early(c):
        for a in range(4):
            swap(c, a).wait_send()
        own(c, lambda copy: copy.wait_send())
        kv(c).wait_send()
        qd(c).wait_send()
        stat(c, 1).wait_send()
        stat(c, 2).wait_send()
        give(c, 0).wait()
        put(c, 0).wait()

    def sent_late(c):
        for a in (1, 2):
            give(c, a).wait()
            put(c, a).wait()

        @pl.when(head(c) != me)
        def _():
            gain(c, level).wait_send()

    def gains_across():
        owner = me // chunks

        @pl.when(owner == side)
        def _():
            grecv[level] = gsend[me - side * chunks]

        def gain_wait(z, carry):
            @pl.when(2 * z + owner != me)
            def _():
                gain(0, z).wait_recv()
            return carry

        lax.fori_loop(0, levels, gain_wait, 0)
        tsend[...] = jnp.sum(grecv[...], axis=0)
        trecv[row] = tsend[...]

        def total_send(p, carry):
            @pl.when(p != row)
            def _():
                total(p, row).start()
            return carry

        lax.fori_loop(0, n_dp, total_send, 0)

    def step(t, carry):
        @pl.when(t + AHEAD < chunks)
        def _():
            swap_start(t + AHEAD)

        @pl.when(t < chunks)
        def _():
            rest(t)

        @pl.when(t + EARLY < chunks)
        def _():
            mine_ready(t + EARLY)
            send_half(t + EARLY, 0)

        @pl.when((t >= FORWARD) & (t < chunks + FORWARD))
        def _():
            forward(t - FORWARD)

        @pl.when(t == FORWARD)
        def _():
            masks()

        @pl.when(t == chunks + QUERIES)
        def _():
            gains_across()

        @pl.when((t >= KEYS) & (t < chunks + KEYS))
        def _():
            keys_side(t - KEYS)

        @pl.when((t >= QUERIES) & (t < chunks + QUERIES))
        def _():
            queries(t - QUERIES)

        @pl.when((t > KEYS) & (t < chunks + KEYS))
        def _():
            sent_early(t - KEYS - 1)
            sent_late(t - KEYS - 1)

        return carry

    lax.fori_loop(0, chunks + KEYS, step, 0)

    def total_wait(p, carry):
        @pl.when(p != row)
        def _():
            total(p, p).wait()
        return carry

    lax.fori_loop(0, n_dp, total_wait, 0)
    sums = jnp.sum(trecv[...], axis=0)
    sublane = lax.broadcasted_iota(jnp.int32, (8, HD), 0)
    tsend[...] = jnp.where(sublane == 0, sums, sums / gk_ref[pl.ds(me, 1), :])
    finals = [
        pltpu.make_async_copy(tsend.at[0:1], gq_out, small_s.at[0]),
        pltpu.make_async_copy(tsend.at[1:2], gk_out, small_s.at[1]),
    ]
    for copy in finals:
        copy.start()
    sent_early(chunks - 1)
    sent_late(chunks - 1)
    for copy in finals:
        copy.wait()


def hand_over(arrays):
    n = len(arrays)

    def move(*refs):
        sources, targets, rooms, sems = refs[:n], refs[n:2 * n], refs[2 * n:3 * n], refs[3 * n]
        loads = [pltpu.make_async_copy(sources[i], rooms[i], sems.at[0, i]) for i in range(n)]
        stores = [pltpu.make_async_copy(rooms[i], targets[i], sems.at[1, i]) for i in range(n)]
        for load in loads:
            load.start()
        for load, store in zip(loads, stores):
            load.wait()
            store.start()
        for store in stores:
            store.wait()

    anywhere = pl.BlockSpec(memory_space=pl.ANY)
    return pl.pallas_call(
        move,
        out_shape=tuple(jax.ShapeDtypeStruct(a.shape, a.dtype) for a in arrays),
        in_specs=[anywhere] * n,
        out_specs=(anywhere,) * n,
        scratch_shapes=[pltpu.VMEM(a.shape, a.dtype) for a in arrays] + [pltpu.SemaphoreType.DMA((2, n))],
        compiler_params=pltpu.CompilerParams(vmem_limit_bytes=60 * 1024 * 1024),
    )(*arrays)


def body(query_states, key_states, value_states, out_grad, doc_ids, query_gain, key_gain):
    n_seq = lax.axis_size("seq")
    n_dp = lax.axis_size("dp")
    rows, feature = query_states.shape[1:]
    heads = feature // HD
    chunks = heads // 2
    window = (chunks, SLOTS, 2, 2, BLOCK, HD)
    dma = pltpu.SemaphoreType.DMA
    anywhere = pl.BlockSpec(memory_space=pl.ANY)
    grad = jax.ShapeDtypeStruct((rows, feature), jnp.bfloat16)
    gain = jax.ShapeDtypeStruct((1, HD), jnp.float32)
    pairs = heads * rows * SPAN
    outs = pl.pallas_call(
        functools.partial(kernel, n_seq, n_dp, heads),
        out_shape=(grad, grad, grad, gain, gain),
        in_specs=[anywhere] * 7,
        out_specs=(anywhere,) * 5,
        scratch_shapes=[
            pltpu.VMEM((heads, HD), jnp.float32),
            pltpu.VMEM((heads, HD), jnp.float32),
            pltpu.VMEM((1, BLOCK), jnp.int32),
            pltpu.VMEM((chunks, 2, 2, BLOCK, HD), jnp.bfloat16),
            pltpu.VMEM(window, jnp.bfloat16),
            pltpu.VMEM(window, jnp.bfloat16),
            pltpu.VMEM((chunks, 3, 2, BLOCK, HD), jnp.bfloat16),
            pltpu.VMEM((4 * REACH + 2, 8, BLOCK), jnp.float32),
            pltpu.VMEM((chunks, SLOTS, 8, PAIR), jnp.float32),
            pltpu.VMEM((2, BLOCK, SPAN), jnp.float32),
            pltpu.VMEM((2, BLOCK, SPAN), jnp.float32),
            pltpu.VMEM((chunks, 8, HD), jnp.float32),
            pltpu.VMEM((n_seq // 2, 8, HD), jnp.float32),
            pltpu.VMEM((8, HD), jnp.float32),
            pltpu.VMEM((n_dp, 8, HD), jnp.float32),
            dma((chunks, 4)), dma((chunks, 4)), dma((chunks, 4)),
            dma((chunks, SLOTS)), dma((chunks, SLOTS)),
            dma((chunks, SLOTS)), dma((chunks, SLOTS)),
            dma((chunks, SLOTS)), dma((chunks, SLOTS)),
            dma((chunks, 3)), dma((chunks, 3)), dma((chunks, 3)),
            dma((4 * REACH + 2,)), dma((4 * REACH + 2,)),
            dma((chunks,)), dma((n_seq // 2,)),
            dma((n_dp,)), dma((n_dp,)), dma((3,)),
        ],
        cost_estimate=pl.CostEstimate(
            flops=14 * pairs * HD, bytes_accessed=7 * rows * feature * 2, transcendentals=2 * pairs
        ),
        compiler_params=pltpu.CompilerParams(
            collective_id=0, has_side_effects=True, vmem_limit_bytes=60 * 1024 * 1024
        ),
    )(
        query_states[0], key_states[0], value_states[0], out_grad[0], doc_ids,
        query_gain.reshape(heads, HD), key_gain.reshape(heads, HD),
    )
    dq, dk, dv, gq, gk = hand_over(outs)
    return (dq[None], dk[None], dv[None], gq[0], gk[0])


def solution(mesh):
    split = P("dp", "seq", None)
    return jax.shard_map(
        body,
        mesh=mesh,
        in_specs=(split, split, split, split, P("dp", "seq"), P(), P()),
        out_specs=(split, split, split, P("seq"), P("seq")),
        check_vma=False,
    )
```

```python
import functools

import jax
import jax.numpy as jnp
from jax import lax
from jax.experimental import pallas as pl
from jax.experimental.pallas import tpu as pltpu
from jax.sharding import PartitionSpec as P

HD = 128
EPS = 1e-06
MASKED = -1e30
LOG2E = 1.4426950408889634
SCALE = HD ** (-0.5)

BLOCK = 128
PAIR = 2 * BLOCK
REACH = 2
SLOTS = REACH + 1
SPAN = 5 * BLOCK
MESH = pl.DeviceIdType.MESH
AHEAD, EARLY, FORWARD, QUERIES, KEYS = 4, 4, 2, 3, 5


def dot_nt(a, b):
    return lax.dot_general(a, b, (((1,), (1,)), ((), ())), preferred_element_type=jnp.float32)


def dot_nn(a, b):
    return lax.dot_general(a, b, (((1,), (0,)), ((), ())), preferred_element_type=jnp.float32)


def inverse_rms(x):
    return lax.rsqrt(jnp.mean(x * x, axis=-1, keepdims=True) + EPS)


def kernel(
    n_seq, n_dp, heads,
    q_ref, k_ref, v_ref, d_ref, doc_any, gq_any, gk_any,
    dq_out, dk_out, dv_out, trecv,
    gq_ref, gk_ref, doc_ref, raw, kvw, qdw, outw, docw, statw, bias_q, bias_k,
    score_q, dprob_q, score_k, dprob_k, gsend, grecv, tsend,
    x_s, x_r, x_l, kv_s, kv_r, qd_s, qd_r, stat_s, stat_r, out_s, out_r, out_l,
    doc_s, doc_r, gain_s, gain_r, tot_s, tot_r, small_s,
):
    me = lax.axis_index("seq")
    row = lax.axis_index("dp")
    side = lax.rem(me, 2)
    level = me // 2
    levels = n_seq // 2
    partner = me + 1 - 2 * side
    chunks = heads // 2
    mine, theirs = side, 1 - side

    def along(dz):
        return lax.rem(me + 2 * dz + n_seq, n_seq)

    def remote(src, dst, send, recv, device):
        return pltpu.make_async_remote_copy(
            src_ref=src, dst_ref=dst, send_sem=send, recv_sem=recv,
            device_id=device, device_id_type=MESH,
        )

    def lanes(h):
        return pl.ds(pl.multiple_of(h * HD, HD), HD)

    def head(c):
        return side * chunks + c

    def other(c):
        return (1 - side) * chunks + c

    sources = (q_ref, k_ref, v_ref, d_ref)
    results = (dq_out, dk_out, dv_out)

    def landing(c, a):
        if a < 2:
            return raw.at[c, side, a]
        if a == 2:
            return kvw.at[c, REACH, side, 1]
        return qdw.at[c, 0, side, 1]

    def swap(c, a):
        return remote(
            sources[a].at[:, lanes(other(c))], landing(c, a), x_s.at[c, a], x_r.at[c, a], {"seq": partner}
        )

    def keep(c, a):
        return pltpu.make_async_copy(sources[a].at[:, lanes(head(c))], landing(c, a), x_l.at[c, a])

    def kv(c):
        return remote(kvw.at[c, 1], kvw.at[c, 0], kv_s.at[c, 2], kv_r.at[c, 2], {"seq": along(1)})

    def qd(c):
        return remote(qdw.at[c, 1], qdw.at[c, 2], qd_s.at[c, 2], qd_r.at[c, 2], {"seq": along(-1)})

    def kv_half(c, i):
        half = (mine, theirs)[i]
        return remote(kvw.at[c, 2, half], kvw.at[c, 1, half], kv_s.at[c, i], kv_r.at[c, i], {"seq": along(1)})

    def qd_half(c, i):
        half = (mine, theirs)[i]
        return remote(qdw.at[c, 0, half], qdw.at[c, 1, half], qd_s.at[c, i], qd_r.at[c, i], {"seq": along(-1)})

    def own(c, act):
        for i in range(2):
            act(kv_half(c, i))
            act(qd_half(c, i))

    def stat(c, t):
        return remote(statw.at[c, 0], statw.at[c, t], stat_s.at[c, t], stat_r.at[c, t], {"seq": along(-t)})

    def give(c, a):
        return remote(
            outw.at[c, a, theirs], results[a].at[:, lanes(head(c))], out_s.at[c, a], out_r.at[c, a],
            {"seq": partner},
        )

    def put(c, a):
        return pltpu.make_async_copy(outw.at[c, a, mine], results[a].at[:, lanes(head(c))], out_l.at[c, a])

    near = [(dz, flip) for dz in range(-REACH, REACH + 1) for flip in (0, 1) if (dz, flip) != (0, 0)]

    def doc(dz, flip):
        there = side + flip - 2 * side * flip
        target = lax.rem(me - side + there + 2 * dz + n_seq, n_seq)
        slot = 2 * (REACH - dz) + side
        return remote(docw.at[2 * REACH + side], docw.at[slot], doc_s.at[2 * (dz + REACH) + flip],
                      doc_r.at[slot], {"seq": target})

    def doc_arrived(dz, flip):
        there = side + flip - 2 * side * flip
        slot = 2 * (REACH + dz) + there
        return remote(docw.at[slot], docw.at[slot], doc_s.at[slot], doc_r.at[slot], {"seq": partner})

    def gain(c, source):
        return remote(gsend.at[c], grecv.at[source], gain_s.at[c], gain_r.at[source], {"seq": head(c)})

    def total(p, source):
        return remote(tsend, trecv.at[source], tot_s.at[p], tot_r.at[source], {"dp": p})

    barrier = pltpu.get_barrier_semaphore()

    for o in range(1, n_seq):
        pl.semaphore_signal(barrier, inc=1, device_id={"seq": lax.rem(me + o, n_seq)}, device_id_type=MESH)
    for o in range(1, n_dp):
        pl.semaphore_signal(barrier, inc=1, device_id={"dp": lax.rem(row + o, n_dp)}, device_id_type=MESH)
    small = [
        pltpu.make_async_copy(src, dst, small_s.at[i])
        for i, (src, dst) in enumerate(((gq_any, gq_ref), (gk_any, gk_ref), (doc_any, doc_ref)))
    ]
    for copy in small:
        copy.start()

    def keep_all(c, carry):
        for a in range(4):
            keep(c, a).start()
        return carry

    def normed(x, gains, h):
        x = x.astype(jnp.float32)
        return (x * inverse_rms(x) * gains[pl.ds(h, 1), :]).astype(jnp.bfloat16)

    def norm_half(c, half):
        kvw[c, REACH, half, 0] = normed(raw[c, half, 1], gk_ref, head(c))
        qdw[c, 0, half, 0] = normed(raw[c, half, 0], gq_ref, head(c))

    def mine_ready(c):
        for a in range(4):
            keep(c, a).wait()
        norm_half(c, mine)

    def send_half(c, i):
        kv_half(c, i).start()
        qd_half(c, i).start()

    def swap_start(c):
        for a in (1, 2, 0, 3):
            swap(c, a).start()

    lax.fori_loop(0, chunks, keep_all, 0)
    for copy in small:
        copy.wait()
    docw[2 * REACH + side] = jnp.broadcast_to(doc_ref[...].astype(jnp.float32), (8, BLOCK))
    for c in range(EARLY):
        mine_ready(c)
    pl.semaphore_wait(barrier, n_seq - 1 + n_dp - 1)
    for c in range(AHEAD):
        swap_start(c)
    for c in range(EARLY):
        send_half(c, 0)
    for dz, flip in near:
        doc(dz, flip).start()

    def rest(c):
        for a in range(4):
            swap(c, a).wait_recv()
        norm_half(c, theirs)
        send_half(c, 1)

    def forward(c):
        own(c, lambda copy: copy.wait_recv())
        kv(c).start()
        qd(c).start()

    def masks():
        for dz, flip in near:
            doc_arrived(dz, flip).wait_recv()
            doc(dz, flip).wait_send()
        rows = lax.broadcasted_iota(jnp.int32, (BLOCK, BLOCK), 0)
        cols = lax.broadcasted_iota(jnp.int32, (BLOCK, BLOCK), 1)
        middle = 2 * REACH
        for sub in range(2):
            own = jnp.broadcast_to(docw[middle + sub, 0:1, :], (BLOCK, BLOCK)).T
            for j in range(5):
                slot = sub + j
                ids = jnp.where(level + slot // 2 - REACH >= 0, docw[slot, 0:1, :], -1.0)
                allowed = own == ids
                if slot == middle + sub:
                    allowed = allowed & (cols <= rows)
                bias_q[sub, :, j * BLOCK:(j + 1) * BLOCK] = jnp.where(allowed, 0.0, MASKED)
                slot = middle + sub + j
                ids = jnp.where(level + slot // 2 - REACH < levels, docw[slot, 0:1, :], -1.0)
                allowed = own == ids
                if j == 0:
                    allowed = allowed & (rows <= cols)
                bias_k[sub, :, j * BLOCK:(j + 1) * BLOCK] = jnp.where(allowed, 0.0, MASKED)

    def norm_back(x, gains, h, grad):
        x = x.astype(jnp.float32)
        rec = inverse_rms(x)
        hat = x * rec
        scaled = grad * gains[pl.ds(h, 1), :]
        back = rec * (scaled - hat * jnp.mean(scaled * hat, axis=-1, keepdims=True))
        return back.astype(jnp.bfloat16), jnp.sum(grad * hat, axis=0, keepdims=True)

    def window(ref, c, a, sub, start=0, stop=5):
        parts = [ref[c, (sub + j) // 2, lax.rem(sub + j, 2), a] for j in range(start, stop)]
        return jnp.concatenate(parts, axis=0)

    def queries_early(c):
        for sub in range(2):
            start = 2 - sub
            cols = pl.ds(start * BLOCK, SPAN - start * BLOCK)
            keys = window(kvw, c, 0, sub, start)
            s = dot_nt(qdw[c, 0, sub, 0], keys) * (SCALE * LOG2E)
            score_q[sub, :, cols] = s + bias_q[sub, :, cols]
            dprob_q[sub, :, cols] = dot_nt(qdw[c, 0, sub, 1], window(kvw, c, 1, sub, start))

    def queries(c):
        queries_early(c)
        kv(c).wait_recv()
        lane = lax.broadcasted_iota(jnp.int32, (BLOCK, BLOCK), 1)
        parts = []
        for sub in range(2):
            start = 2 - sub
            cols = pl.ds(0, start * BLOCK)
            keys = window(kvw, c, 0, sub, 0, start)
            s = dot_nt(qdw[c, 0, sub, 0], keys) * (SCALE * LOG2E)
            score_q[sub, :, cols] = s + bias_q[sub, :, cols]
            dprob_q[sub, :, cols] = dot_nt(qdw[c, 0, sub, 1], window(kvw, c, 1, sub, 0, start))
            s = score_q[sub]
            dprob = dprob_q[sub]
            peak = jnp.max(s, axis=1, keepdims=True)
            e = jnp.exp2(s - peak)
            weight = jnp.sum(e, axis=1, keepdims=True)
            inv = 1.0 / weight
            delta = jnp.sum(e * dprob, axis=1, keepdims=True) * inv
            stats = jnp.where(lane == 0, peak + jnp.log2(weight), delta)
            statw[c, 0, :, sub * BLOCK:(sub + 1) * BLOCK] = stats.T[0:8]
            score_q[sub] = e
            parts.append((inv, delta))
        for t in range(1, SLOTS):
            stat(c, t).start()
        terms, key_terms = [], []
        for sub in range(2):
            inv, delta = parts[sub]
            dscore = (score_q[sub] * (inv * SCALE) * (dprob_q[sub] - delta)).astype(jnp.bfloat16)
            grad = dot_nn(dscore, window(kvw, c, 0, sub))
            back, term = norm_back(raw[c, sub, 0], gq_ref, head(c), grad)
            outw[c, 0, sub] = back
            terms.append(term)
            key_terms.append(jnp.sum(grad * qdw[c, 0, sub, 0].astype(jnp.float32), axis=0, keepdims=True))
        sublane = lax.broadcasted_iota(jnp.int32, (8, HD), 0)
        key_term = (key_terms[0] + key_terms[1]) / gk_ref[pl.ds(head(c), 1), :]
        gsend[c] = jnp.where(sublane == 0, terms[0] + terms[1], key_term)

        @pl.when(head(c) != me)
        def _():
            gain(c, level).start()

        give(c, 0).start()
        put(c, 0).start()

    def keys_side(c):
        qd(c).wait_recv()
        for sub in range(2):
            s = dot_nt(kvw[c, REACH, sub, 0], window(qdw, c, 0, sub)) * (SCALE * LOG2E)
            score_k[sub] = s + bias_k[sub]
            dprob_k[sub] = dot_nt(kvw[c, REACH, sub, 1], window(qdw, c, 1, sub))
        for t in range(1, SLOTS):
            stat(c, t).wait_recv()

        def stat_row(r, sub):
            parts = [
                statw[c, (sub + j) // 2, r:r + 1, pl.ds(pl.multiple_of(lax.rem(sub + j, 2) * BLOCK, BLOCK), BLOCK)]
                for j in range(5)
            ]
            return jnp.concatenate(parts, axis=1)

        for i, sub in enumerate((theirs, mine)):
            p = jnp.exp2(score_k[sub] - stat_row(0, sub))
            dv = dot_nn(p.astype(jnp.bfloat16), window(qdw, c, 1, sub))
            outw[c, 2, sub] = dv.astype(jnp.bfloat16)
            if i == 0:
                give(c, 2).start()
            dscore = (p * SCALE * (dprob_k[sub] - stat_row(1, sub))).astype(jnp.bfloat16)
            grad = dot_nn(dscore, window(qdw, c, 0, sub))
            outw[c, 1, sub], _ = norm_back(raw[c, sub, 1], gk_ref, head(c), grad)
            if i == 0:
                give(c, 1).start()
        for a in (1, 2):
            put(c, a).start()

    def sent_early(c):
        for a in range(4):
            swap(c, a).wait_send()
        own(c, lambda copy: copy.wait_send())
        kv(c).wait_send()
        qd(c).wait_send()
        stat(c, 1).wait_send()
        stat(c, 2).wait_send()
        give(c, 0).wait()
        put(c, 0).wait()

    def sent_late(c):
        for a in (1, 2):
            give(c, a).wait()
            put(c, a).wait()

        @pl.when(head(c) != me)
        def _():
            gain(c, level).wait_send()

    def gains_across():
        owner = me // chunks

        @pl.when(owner == side)
        def _():
            grecv[level] = gsend[me - side * chunks]

        def gain_wait(z, carry):
            @pl.when(2 * z + owner != me)
            def _():
                gain(0, z).wait_recv()
            return carry

        lax.fori_loop(0, levels, gain_wait, 0)
        tsend[...] = jnp.sum(grecv[...], axis=0)
        pltpu.make_async_copy(tsend, trecv.at[row], small_s.at[0]).start()

        def total_send(p, carry):
            @pl.when(p != row)
            def _():
                total(p, row).start()
            return carry

        lax.fori_loop(0, n_dp, total_send, 0)

    def step(t, carry):
        @pl.when(t + AHEAD < chunks)
        def _():
            swap_start(t + AHEAD)

        @pl.when(t < chunks)
        def _():
            rest(t)

        @pl.when(t + EARLY < chunks)
        def _():
            mine_ready(t + EARLY)
            send_half(t + EARLY, 0)

        @pl.when((t >= FORWARD) & (t < chunks + FORWARD))
        def _():
            forward(t - FORWARD)

        @pl.when(t == FORWARD)
        def _():
            masks()

        @pl.when(t == chunks + QUERIES)
        def _():
            gains_across()

        @pl.when((t >= KEYS) & (t < chunks + KEYS))
        def _():
            keys_side(t - KEYS)

        @pl.when((t >= QUERIES) & (t < chunks + QUERIES))
        def _():
            queries(t - QUERIES)

        @pl.when((t > KEYS) & (t < chunks + KEYS))
        def _():
            sent_early(t - KEYS - 1)
            sent_late(t - KEYS - 1)

        return carry

    lax.fori_loop(0, chunks + KEYS, step, 0)

    def total_wait(p, carry):
        @pl.when(p != row)
        def _():
            total(p, p).wait()
        return carry

    lax.fori_loop(0, n_dp, total_wait, 0)
    pltpu.make_async_copy(tsend, trecv.at[row], small_s.at[0]).wait()
    sent_early(chunks - 1)
    sent_late(chunks - 1)


def hand_over(arrays, totals):
    n = len(arrays)

    def move(*refs):
        sources, totals_ref = refs[:n], refs[n]
        targets, gains = refs[n + 1:2 * n + 1], refs[2 * n + 1:2 * n + 3]
        rooms, totals_room, sums, sems = refs[2 * n + 3:3 * n + 3], refs[-3], refs[-2], refs[-1]
        loads = [pltpu.make_async_copy(totals_ref, totals_room, sems.at[0, n])]
        loads += [pltpu.make_async_copy(sources[i], rooms[i], sems.at[0, i]) for i in range(n)]
        stores = [pltpu.make_async_copy(sums.at[i:i + 1], gains[i], sems.at[1, n + i]) for i in range(2)]
        stores += [pltpu.make_async_copy(rooms[i], targets[i], sems.at[1, i]) for i in range(n)]
        for load in loads:
            load.start()
        loads[0].wait()
        sums[...] = jnp.sum(totals_room[...], axis=0)
        for store in stores[:2]:
            store.start()
        for load, store in zip(loads[1:], stores[2:]):
            load.wait()
            store.start()
        for store in stores:
            store.wait()

    anywhere = pl.BlockSpec(memory_space=pl.ANY)
    gain = jax.ShapeDtypeStruct((1, HD), jnp.float32)
    return pl.pallas_call(
        move,
        out_shape=tuple(jax.ShapeDtypeStruct(a.shape, a.dtype) for a in arrays) + (gain, gain),
        in_specs=[anywhere] * (n + 1),
        out_specs=(anywhere,) * (n + 2),
        scratch_shapes=[pltpu.VMEM(a.shape, a.dtype) for a in arrays]
        + [pltpu.VMEM(totals.shape, totals.dtype), pltpu.VMEM((8, HD), jnp.float32)]
        + [pltpu.SemaphoreType.DMA((2, n + 2))],
        compiler_params=pltpu.CompilerParams(vmem_limit_bytes=60 * 1024 * 1024),
    )(*arrays, totals)


def body(query_states, key_states, value_states, out_grad, doc_ids, query_gain, key_gain):
    n_seq = lax.axis_size("seq")
    n_dp = lax.axis_size("dp")
    rows, feature = query_states.shape[1:]
    heads = feature // HD
    chunks = heads // 2
    window = (chunks, SLOTS, 2, 2, BLOCK, HD)
    dma = pltpu.SemaphoreType.DMA
    anywhere = pl.BlockSpec(memory_space=pl.ANY)
    grad = jax.ShapeDtypeStruct((rows, feature), jnp.bfloat16)
    totals = jax.ShapeDtypeStruct((n_dp, 8, HD), jnp.float32)
    pairs = heads * rows * SPAN
    outs = pl.pallas_call(
        functools.partial(kernel, n_seq, n_dp, heads),
        out_shape=(grad, grad, grad, totals),
        in_specs=[anywhere] * 7,
        out_specs=(anywhere,) * 4,
        scratch_shapes=[
            pltpu.VMEM((heads, HD), jnp.float32),
            pltpu.VMEM((heads, HD), jnp.float32),
            pltpu.VMEM((1, BLOCK), jnp.int32),
            pltpu.VMEM((chunks, 2, 2, BLOCK, HD), jnp.bfloat16),
            pltpu.VMEM(window, jnp.bfloat16),
            pltpu.VMEM(window, jnp.bfloat16),
            pltpu.VMEM((chunks, 3, 2, BLOCK, HD), jnp.bfloat16),
            pltpu.VMEM((4 * REACH + 2, 8, BLOCK), jnp.float32),
            pltpu.VMEM((chunks, SLOTS, 8, PAIR), jnp.float32),
            pltpu.VMEM((2, BLOCK, SPAN), jnp.float32),
            pltpu.VMEM((2, BLOCK, SPAN), jnp.float32),
            pltpu.VMEM((2, BLOCK, SPAN), jnp.float32),
            pltpu.VMEM((2, BLOCK, SPAN), jnp.float32),
            pltpu.VMEM((2, BLOCK, SPAN), jnp.float32),
            pltpu.VMEM((2, BLOCK, SPAN), jnp.float32),
            pltpu.VMEM((chunks, 8, HD), jnp.float32),
            pltpu.VMEM((n_seq // 2, 8, HD), jnp.float32),
            pltpu.VMEM((8, HD), jnp.float32),
            dma((chunks, 4)), dma((chunks, 4)), dma((chunks, 4)),
            dma((chunks, SLOTS)), dma((chunks, SLOTS)),
            dma((chunks, SLOTS)), dma((chunks, SLOTS)),
            dma((chunks, SLOTS)), dma((chunks, SLOTS)),
            dma((chunks, 3)), dma((chunks, 3)), dma((chunks, 3)),
            dma((4 * REACH + 2,)), dma((4 * REACH + 2,)),
            dma((chunks,)), dma((n_seq // 2,)),
            dma((n_dp,)), dma((n_dp,)), dma((3,)),
        ],
        cost_estimate=pl.CostEstimate(
            flops=14 * pairs * HD, bytes_accessed=7 * rows * feature * 2, transcendentals=2 * pairs
        ),
        compiler_params=pltpu.CompilerParams(
            collective_id=0, has_side_effects=True, vmem_limit_bytes=60 * 1024 * 1024
        ),
    )(
        query_states[0], key_states[0], value_states[0], out_grad[0], doc_ids,
        query_gain.reshape(heads, HD), key_gain.reshape(heads, HD),
    )
    dq, dk, dv, gq, gk = hand_over(outs[:3], outs[3])
    return (dq[None], dk[None], dv[None], gq[0], gk[0])


def solution(mesh):
    split = P("dp", "seq", None)
    return jax.shard_map(
        body,
        mesh=mesh,
        in_specs=(split, split, split, split, P("dp", "seq"), P(), P()),
        out_specs=(split, split, split, P("seq"), P("seq")),
        check_vma=False,
    )
```

```python
import functools

import jax
import jax.numpy as jnp
from jax import lax
from jax.experimental import pallas as pl
from jax.experimental.pallas import tpu as pltpu
from jax.sharding import PartitionSpec as P

HD = 128
EPS = 1e-06
MASKED = -1e30
LOG2E = 1.4426950408889634
SCALE = HD ** (-0.5)

BLOCK = 128
PAIR = 2 * BLOCK
REACH = 2
SLOTS = REACH + 1
SPAN = 5 * BLOCK
MESH = pl.DeviceIdType.MESH
AHEAD, EARLY, FORWARD, QUERIES, KEYS = 4, 4, 2, 3, 5


def dot_nt(a, b):
    return lax.dot_general(a, b, (((1,), (1,)), ((), ())), preferred_element_type=jnp.float32)


def dot_nn(a, b):
    return lax.dot_general(a, b, (((1,), (0,)), ((), ())), preferred_element_type=jnp.float32)


def inverse_rms(x):
    return lax.rsqrt(jnp.mean(x * x, axis=-1, keepdims=True) + EPS)


def kernel(
    n_seq, n_dp, heads,
    q_ref, k_ref, v_ref, d_ref, doc_any, gq_any, gk_any,
    dq_out, dk_out, dv_out, trecv,
    gq_ref, gk_ref, doc_ref, raw, kvw, qdw, outw, docw, statw, bias_q, bias_k,
    score_q, dprob_q, score_k, dprob_k, gsend, grecv, tsend,
    x_s, x_r, x_l, kv_s, kv_r, qd_s, qd_r, stat_s, stat_r, out_s, out_r, out_l,
    doc_s, doc_r, gain_s, gain_r, tot_s, tot_r, small_s,
):
    me = lax.axis_index("seq")
    row = lax.axis_index("dp")
    side = lax.rem(me, 2)
    level = me // 2
    levels = n_seq // 2
    partner = me + 1 - 2 * side
    chunks = heads // 2
    mine, theirs = side, 1 - side

    def along(dz):
        return lax.rem(me + 2 * dz + n_seq, n_seq)

    def remote(src, dst, send, recv, device):
        return pltpu.make_async_remote_copy(
            src_ref=src, dst_ref=dst, send_sem=send, recv_sem=recv,
            device_id=device, device_id_type=MESH,
        )

    def lanes(h):
        return pl.ds(pl.multiple_of(h * HD, HD), HD)

    def head(c):
        return side * chunks + c

    def other(c):
        return (1 - side) * chunks + c

    sources = (q_ref, k_ref, v_ref, d_ref)
    results = (dq_out, dk_out, dv_out)

    def landing(c, a):
        if a < 2:
            return raw.at[c, side, a]
        if a == 2:
            return kvw.at[c, REACH, side, 1]
        return qdw.at[c, 0, side, 1]

    def swap(c, a):
        return remote(
            sources[a].at[:, lanes(other(c))], landing(c, a), x_s.at[c, a], x_r.at[c, a], {"seq": partner}
        )

    def keep(c, a):
        return pltpu.make_async_copy(sources[a].at[:, lanes(head(c))], landing(c, a), x_l.at[c, a])

    def kv(c):
        return remote(kvw.at[c, 1], kvw.at[c, 0], kv_s.at[c, 2], kv_r.at[c, 2], {"seq": along(1)})

    def qd(c):
        return remote(qdw.at[c, 1], qdw.at[c, 2], qd_s.at[c, 2], qd_r.at[c, 2], {"seq": along(-1)})

    def kv_half(c, i):
        half = (mine, theirs)[i]
        return remote(kvw.at[c, 2, half], kvw.at[c, 1, half], kv_s.at[c, i], kv_r.at[c, i], {"seq": along(1)})

    def qd_half(c, i):
        half = (mine, theirs)[i]
        return remote(qdw.at[c, 0, half], qdw.at[c, 1, half], qd_s.at[c, i], qd_r.at[c, i], {"seq": along(-1)})

    def own(c, act):
        for i in range(2):
            act(kv_half(c, i))
            act(qd_half(c, i))

    def stat(c, t):
        return remote(statw.at[c, 0], statw.at[c, t], stat_s.at[c, t], stat_r.at[c, t], {"seq": along(-t)})

    def give(c, a):
        return remote(
            outw.at[c, a, theirs], results[a].at[:, lanes(head(c))], out_s.at[c, a], out_r.at[c, a],
            {"seq": partner},
        )

    def put(c, a):
        return pltpu.make_async_copy(outw.at[c, a, mine], results[a].at[:, lanes(head(c))], out_l.at[c, a])

    near = [(dz, flip) for dz in range(-REACH, REACH + 1) for flip in (0, 1) if (dz, flip) != (0, 0)]

    def doc(dz, flip):
        there = side + flip - 2 * side * flip
        target = lax.rem(me - side + there + 2 * dz + n_seq, n_seq)
        slot = 2 * (REACH - dz) + side
        return remote(docw.at[2 * REACH + side], docw.at[slot], doc_s.at[2 * (dz + REACH) + flip],
                      doc_r.at[slot], {"seq": target})

    def doc_arrived(dz, flip):
        there = side + flip - 2 * side * flip
        slot = 2 * (REACH + dz) + there
        return remote(docw.at[slot], docw.at[slot], doc_s.at[slot], doc_r.at[slot], {"seq": partner})

    def gain(c, source):
        return remote(gsend.at[c], grecv.at[source], gain_s.at[c], gain_r.at[source], {"seq": head(c)})

    def total(p, source):
        return remote(tsend, trecv.at[source], tot_s.at[p], tot_r.at[source], {"dp": p})

    barrier = pltpu.get_barrier_semaphore()

    for o in range(1, n_seq):
        pl.semaphore_signal(barrier, inc=1, device_id={"seq": lax.rem(me + o, n_seq)}, device_id_type=MESH)
    for o in range(1, n_dp):
        pl.semaphore_signal(barrier, inc=1, device_id={"dp": lax.rem(row + o, n_dp)}, device_id_type=MESH)
    small = [
        pltpu.make_async_copy(src, dst, small_s.at[i])
        for i, (src, dst) in enumerate(((gq_any, gq_ref), (gk_any, gk_ref), (doc_any, doc_ref)))
    ]
    for copy in small:
        copy.start()

    def keep_all(c, carry):
        for a in range(4):
            keep(c, a).start()
        return carry

    def normed(x, gains, h):
        x = x.astype(jnp.float32)
        return (x * inverse_rms(x) * gains[pl.ds(h, 1), :]).astype(jnp.bfloat16)

    def norm_half(c, half):
        kvw[c, REACH, half, 0] = normed(raw[c, half, 1], gk_ref, head(c))
        qdw[c, 0, half, 0] = normed(raw[c, half, 0], gq_ref, head(c))

    def mine_ready(c):
        for a in range(4):
            keep(c, a).wait()
        norm_half(c, mine)

    def send_half(c, i):
        kv_half(c, i).start()
        qd_half(c, i).start()

    def swap_start(c):
        for a in (1, 2, 0, 3):
            swap(c, a).start()

    lax.fori_loop(0, chunks, keep_all, 0)
    for copy in small:
        copy.wait()
    docw[2 * REACH + side] = doc_ref[...].astype(jnp.float32)
    for c in range(EARLY):
        mine_ready(c)
    pl.semaphore_wait(barrier, n_seq - 1 + n_dp - 1)
    for c in range(AHEAD):
        swap_start(c)
    for c in range(EARLY):
        send_half(c, 0)
    for dz, flip in near:
        doc(dz, flip).start()

    def rest(c):
        for a in range(4):
            swap(c, a).wait_recv()
        norm_half(c, theirs)
        send_half(c, 1)

    def forward(c):
        own(c, lambda copy: copy.wait_recv())
        kv(c).start()
        qd(c).start()

    def masks():
        for dz, flip in near:
            doc_arrived(dz, flip).wait_recv()
            doc(dz, flip).wait_send()
        rows = lax.broadcasted_iota(jnp.int32, (BLOCK, BLOCK), 0)
        cols = lax.broadcasted_iota(jnp.int32, (BLOCK, BLOCK), 1)
        middle = 2 * REACH
        for sub in range(2):
            own = jnp.broadcast_to(docw[middle + sub, 0:1, :], (BLOCK, BLOCK)).T
            for j in range(5):
                slot = sub + j
                ids = jnp.where(level + slot // 2 - REACH >= 0, docw[slot, 0:1, :], -1.0)
                allowed = own == ids
                if slot == middle + sub:
                    allowed = allowed & (cols <= rows)
                bias_q[sub, :, j * BLOCK:(j + 1) * BLOCK] = jnp.where(allowed, 0.0, MASKED)
                slot = middle + sub + j
                ids = jnp.where(level + slot // 2 - REACH < levels, docw[slot, 0:1, :], -1.0)
                allowed = own == ids
                if j == 0:
                    allowed = allowed & (rows <= cols)
                bias_k[sub, :, j * BLOCK:(j + 1) * BLOCK] = jnp.where(allowed, 0.0, MASKED)

    def norm_back(x, gains, h, grad):
        x = x.astype(jnp.float32)
        rec = inverse_rms(x)
        hat = x * rec
        scaled = grad * gains[pl.ds(h, 1), :]
        back = rec * (scaled - hat * jnp.mean(scaled * hat, axis=-1, keepdims=True))
        return back.astype(jnp.bfloat16), jnp.sum(grad * hat, axis=0, keepdims=True)

    def window(ref, c, a, sub, start=0, stop=5):
        parts = [ref[c, (sub + j) // 2, lax.rem(sub + j, 2), a] for j in range(start, stop)]
        return jnp.concatenate(parts, axis=0)

    def queries_early(c):
        for sub in range(2):
            start = 2 - sub
            cols = pl.ds(start * BLOCK, SPAN - start * BLOCK)
            keys = window(kvw, c, 0, sub, start)
            s = dot_nt(qdw[c, 0, sub, 0], keys) * (SCALE * LOG2E)
            score_q[sub, :, cols] = s + bias_q[sub, :, cols]
            dprob_q[sub, :, cols] = dot_nt(qdw[c, 0, sub, 1], window(kvw, c, 1, sub, start))

    def queries(c):
        queries_early(c)
        kv(c).wait_recv()
        lane = lax.broadcasted_iota(jnp.int32, (BLOCK, BLOCK), 1)
        parts = []
        for sub in range(2):
            start = 2 - sub
            cols = pl.ds(0, start * BLOCK)
            keys = window(kvw, c, 0, sub, 0, start)
            s = dot_nt(qdw[c, 0, sub, 0], keys) * (SCALE * LOG2E)
            score_q[sub, :, cols] = s + bias_q[sub, :, cols]
            dprob_q[sub, :, cols] = dot_nt(qdw[c, 0, sub, 1], window(kvw, c, 1, sub, 0, start))
            s = score_q[sub]
            dprob = dprob_q[sub]
            peak = jnp.max(s, axis=1, keepdims=True)
            e = jnp.exp2(s - peak)
            weight = jnp.sum(e, axis=1, keepdims=True)
            inv = 1.0 / weight
            delta = jnp.sum(e * dprob, axis=1, keepdims=True) * inv
            stats = jnp.where(lane == 0, peak + jnp.log2(weight), delta)
            statw[c, 0, :, sub * BLOCK:(sub + 1) * BLOCK] = stats.T[0:2]
            score_q[sub] = e
            parts.append((inv, delta))
        for t in range(1, SLOTS):
            stat(c, t).start()
        terms, key_terms = [], []
        for sub in range(2):
            inv, delta = parts[sub]
            dscore = (score_q[sub] * (inv * SCALE) * (dprob_q[sub] - delta)).astype(jnp.bfloat16)
            grad = dot_nn(dscore, window(kvw, c, 0, sub))
            back, term = norm_back(raw[c, sub, 0], gq_ref, head(c), grad)
            outw[c, 0, sub] = back
            terms.append(term)
            key_terms.append(jnp.sum(grad * qdw[c, 0, sub, 0].astype(jnp.float32), axis=0, keepdims=True))
        gsend[c, 0:1] = terms[0] + terms[1]
        gsend[c, 1:2] = (key_terms[0] + key_terms[1]) / gk_ref[pl.ds(head(c), 1), :]

        @pl.when(head(c) != me)
        def _():
            gain(c, level).start()

        give(c, 0).start()
        put(c, 0).start()

    def keys_side(c):
        qd(c).wait_recv()
        for sub in range(2):
            s = dot_nt(kvw[c, REACH, sub, 0], window(qdw, c, 0, sub)) * (SCALE * LOG2E)
            score_k[sub] = s + bias_k[sub]
            dprob_k[sub] = dot_nt(kvw[c, REACH, sub, 1], window(qdw, c, 1, sub))
        for t in range(1, SLOTS):
            stat(c, t).wait_recv()

        def stat_row(r, sub):
            parts = [
                statw[c, (sub + j) // 2, r:r + 1, pl.ds(pl.multiple_of(lax.rem(sub + j, 2) * BLOCK, BLOCK), BLOCK)]
                for j in range(5)
            ]
            return jnp.concatenate(parts, axis=1)

        for i, sub in enumerate((theirs, mine)):
            p = jnp.exp2(score_k[sub] - stat_row(0, sub))
            dv = dot_nn(p.astype(jnp.bfloat16), window(qdw, c, 1, sub))
            outw[c, 2, sub] = dv.astype(jnp.bfloat16)
            if i == 0:
                give(c, 2).start()
            dscore = (p * SCALE * (dprob_k[sub] - stat_row(1, sub))).astype(jnp.bfloat16)
            grad = dot_nn(dscore, window(qdw, c, 0, sub))
            outw[c, 1, sub], _ = norm_back(raw[c, sub, 1], gk_ref, head(c), grad)
            if i == 0:
                give(c, 1).start()
        for a in (1, 2):
            put(c, a).start()

    def sent_early(c):
        for a in range(4):
            swap(c, a).wait_send()
        own(c, lambda copy: copy.wait_send())
        kv(c).wait_send()
        qd(c).wait_send()
        stat(c, 1).wait_send()
        stat(c, 2).wait_send()
        give(c, 0).wait()
        put(c, 0).wait()

    def sent_late(c):
        for a in (1, 2):
            give(c, a).wait()
            put(c, a).wait()

        @pl.when(head(c) != me)
        def _():
            gain(c, level).wait_send()

    def gains_across():
        owner = me // chunks

        @pl.when(owner == side)
        def _():
            grecv[level] = gsend[me - side * chunks]

        def gain_wait(z, carry):
            @pl.when(2 * z + owner != me)
            def _():
                gain(0, z).wait_recv()
            return carry

        lax.fori_loop(0, levels, gain_wait, 0)
        tsend[...] = jnp.sum(grecv[...], axis=0)
        pltpu.make_async_copy(tsend, trecv.at[row], small_s.at[0]).start()

        def total_send(p, carry):
            @pl.when(p != row)
            def _():
                total(p, row).start()
            return carry

        lax.fori_loop(0, n_dp, total_send, 0)

    def step(t, carry):
        @pl.when(t + AHEAD < chunks)
        def _():
            swap_start(t + AHEAD)

        @pl.when(t < chunks)
        def _():
            rest(t)

        @pl.when(t + EARLY < chunks)
        def _():
            mine_ready(t + EARLY)
            send_half(t + EARLY, 0)

        @pl.when((t >= FORWARD) & (t < chunks + FORWARD))
        def _():
            forward(t - FORWARD)

        @pl.when(t == FORWARD)
        def _():
            masks()

        @pl.when(t == chunks + QUERIES)
        def _():
            gains_across()

        @pl.when((t >= KEYS) & (t < chunks + KEYS))
        def _():
            keys_side(t - KEYS)

        @pl.when((t >= QUERIES) & (t < chunks + QUERIES))
        def _():
            queries(t - QUERIES)

        @pl.when((t > KEYS) & (t < chunks + KEYS))
        def _():
            sent_early(t - KEYS - 1)
            sent_late(t - KEYS - 1)

        return carry

    lax.fori_loop(0, chunks + KEYS, step, 0)

    def total_wait(p, carry):
        @pl.when(p != row)
        def _():
            total(p, p).wait()
        return carry

    lax.fori_loop(0, n_dp, total_wait, 0)
    pltpu.make_async_copy(tsend, trecv.at[row], small_s.at[0]).wait()
    sent_early(chunks - 1)
    sent_late(chunks - 1)


def hand_over(arrays, totals):
    n = len(arrays)

    def move(*refs):
        sources, totals_ref = refs[:n], refs[n]
        targets, gains = refs[n + 1:2 * n + 1], refs[2 * n + 1:2 * n + 3]
        rooms, totals_room, sums, sems = refs[2 * n + 3:3 * n + 3], refs[-3], refs[-2], refs[-1]
        loads = [pltpu.make_async_copy(totals_ref, totals_room, sems.at[0, n])]
        loads += [pltpu.make_async_copy(sources[i], rooms[i], sems.at[0, i]) for i in range(n)]
        stores = [pltpu.make_async_copy(sums.at[i:i + 1], gains[i], sems.at[1, n + i]) for i in range(2)]
        stores += [pltpu.make_async_copy(rooms[i], targets[i], sems.at[1, i]) for i in range(n)]
        for load in loads:
            load.start()
        loads[0].wait()
        sums[...] = jnp.sum(totals_room[...], axis=0)
        for store in stores[:2]:
            store.start()
        for load, store in zip(loads[1:], stores[2:]):
            load.wait()
            store.start()
        for store in stores:
            store.wait()

    anywhere = pl.BlockSpec(memory_space=pl.ANY)
    gain = jax.ShapeDtypeStruct((1, HD), jnp.float32)
    return pl.pallas_call(
        move,
        out_shape=tuple(jax.ShapeDtypeStruct(a.shape, a.dtype) for a in arrays) + (gain, gain),
        in_specs=[anywhere] * (n + 1),
        out_specs=(anywhere,) * (n + 2),
        scratch_shapes=[pltpu.VMEM(a.shape, a.dtype) for a in arrays]
        + [pltpu.VMEM(totals.shape, totals.dtype), pltpu.VMEM((2, HD), jnp.float32)]
        + [pltpu.SemaphoreType.DMA((2, n + 2))],
        compiler_params=pltpu.CompilerParams(vmem_limit_bytes=60 * 1024 * 1024),
    )(*arrays, totals)


def body(query_states, key_states, value_states, out_grad, doc_ids, query_gain, key_gain):
    n_seq = lax.axis_size("seq")
    n_dp = lax.axis_size("dp")
    rows, feature = query_states.shape[1:]
    heads = feature // HD
    chunks = heads // 2
    window = (chunks, SLOTS, 2, 2, BLOCK, HD)
    dma = pltpu.SemaphoreType.DMA
    anywhere = pl.BlockSpec(memory_space=pl.ANY)
    grad = jax.ShapeDtypeStruct((rows, feature), jnp.bfloat16)
    totals = jax.ShapeDtypeStruct((n_dp, 2, HD), jnp.float32)
    pairs = heads * rows * SPAN
    outs = pl.pallas_call(
        functools.partial(kernel, n_seq, n_dp, heads),
        out_shape=(grad, grad, grad, totals),
        in_specs=[anywhere] * 7,
        out_specs=(anywhere,) * 4,
        scratch_shapes=[
            pltpu.VMEM((heads, HD), jnp.float32),
            pltpu.VMEM((heads, HD), jnp.float32),
            pltpu.VMEM((1, BLOCK), jnp.int32),
            pltpu.VMEM((chunks, 2, 2, BLOCK, HD), jnp.bfloat16),
            pltpu.VMEM(window, jnp.bfloat16),
            pltpu.VMEM(window, jnp.bfloat16),
            pltpu.VMEM((chunks, 3, 2, BLOCK, HD), jnp.bfloat16),
            pltpu.VMEM((4 * REACH + 2, 1, BLOCK), jnp.float32),
            pltpu.VMEM((chunks, SLOTS, 2, PAIR), jnp.float32),
            pltpu.VMEM((2, BLOCK, SPAN), jnp.float32),
            pltpu.VMEM((2, BLOCK, SPAN), jnp.float32),
            pltpu.VMEM((2, BLOCK, SPAN), jnp.float32),
            pltpu.VMEM((2, BLOCK, SPAN), jnp.float32),
            pltpu.VMEM((2, BLOCK, SPAN), jnp.float32),
            pltpu.VMEM((2, BLOCK, SPAN), jnp.float32),
            pltpu.VMEM((chunks, 2, HD), jnp.float32),
            pltpu.VMEM((n_seq // 2, 2, HD), jnp.float32),
            pltpu.VMEM((2, HD), jnp.float32),
            dma((chunks, 4)), dma((chunks, 4)), dma((chunks, 4)),
            dma((chunks, SLOTS)), dma((chunks, SLOTS)),
            dma((chunks, SLOTS)), dma((chunks, SLOTS)),
            dma((chunks, SLOTS)), dma((chunks, SLOTS)),
            dma((chunks, 3)), dma((chunks, 3)), dma((chunks, 3)),
            dma((4 * REACH + 2,)), dma((4 * REACH + 2,)),
            dma((chunks,)), dma((n_seq // 2,)),
            dma((n_dp,)), dma((n_dp,)), dma((3,)),
        ],
        cost_estimate=pl.CostEstimate(
            flops=14 * pairs * HD, bytes_accessed=7 * rows * feature * 2, transcendentals=2 * pairs
        ),
        compiler_params=pltpu.CompilerParams(
            collective_id=0, has_side_effects=True, vmem_limit_bytes=60 * 1024 * 1024
        ),
    )(
        query_states[0], key_states[0], value_states[0], out_grad[0], doc_ids,
        query_gain.reshape(heads, HD), key_gain.reshape(heads, HD),
    )
    dq, dk, dv, gq, gk = hand_over(outs[:3], outs[3])
    return (dq[None], dk[None], dv[None], gq[0], gk[0])


def solution(mesh):
    split = P("dp", "seq", None)
    return jax.shard_map(
        body,
        mesh=mesh,
        in_specs=(split, split, split, split, P("dp", "seq"), P(), P()),
        out_specs=(split, split, split, P("seq"), P("seq")),
        check_vma=False,
    )
```
